768 devices in a mesh: dp: 48 (over y_lo, z, core), context: 16 (over x, y_hi).
Axes of the slice: x: 4, y: 8 (y_hi: 4, y_lo: 2; y = y_hi * 2 + y_lo), z: 12, core: 2. Of those that a mesh axis runs over, the one named last changes fastest.
Arguments:
- tokens: bfloat16 [96, 4096, 768], P('dp', 'context'), may hold values from -6 to 6
- w_in: bfloat16 [768, 768], replicated, may hold values from -0.21875 to 0.21875
- factor_one: bfloat16 [64, 64, 64], P('context'), may hold values from -0.75 to 0.75
- factor_two: bfloat16 [64, 64, 64], P('context'), may hold values from -0.75 to 0.75
- queries: float32 [96, 768], P('dp'), may hold values from -6 to 6
- neg_ids: int32 [96, 8], replicated, may hold values from 0 to 95
- pad_lengths: int32 [96], P('dp'), may hold values from 0 to 2048
Outputs:
- losses: float32 [96], P('dp')
- tokens_grad: float32 [96, 4096, 768], P('dp', 'context')
The draws below stay inside these ranges and needn't reach their ends.
Inputs may be any that keep to these rules, and one draw needn't show every extreme that they name: `neg_ids`: ids of documents of the batch; a few documents are listed very often, repeats and a query's own document included.
All inputs are finite; a program needn't handle non-finite values.
Results may differ from the reference program's by a relative error of at most 0.007.
Values may be sent and summed in bfloat16 or wider, within the bound.
A program may use at most 32 MiB of HBM per device.

```python
import math
import jax
import jax.numpy as jnp
import numpy as np
from jax import lax

D = 768
BLK = 64
NEG = 8
SEQ = 4096
DOCS = 96


def touch_ends(entries, stream_key, low, largest):
    spot = [jax.random.randint(jax.random.fold_in(stream_key, axis), (), 0, length) for axis, length in enumerate(entries.shape)]
    widest = entries.shape.index(max(entries.shape))
    next_to = spot[:widest] + [(spot[widest] + 1) % entries.shape[widest]] + spot[widest + 1:]
    return entries.at[tuple(spot)].set(low).at[tuple(next_to)].set(largest)


def levels(own_key, extent, split, smallest, top_value):
    def one(dim, parts):
        heights = jax.random.uniform(jax.random.fold_in(jax.random.fold_in(own_key, 6), dim), (parts,), jnp.float32, smallest / len(split), top_value / len(split))
        return jnp.repeat(jnp.exp(heights), extent[dim] // parts).reshape((-1,) + (1,) * (len(extent) - dim - 1))

    gain = one(*split[0])
    for cut in split[1:]:
        gain = gain * one(*cut)
    return gain


def cumulative_ranks(number_of, skew):
    weights = [(1 << 20) // math.isqrt(standing ** skew) + 1 for standing in range(1, number_of + 1)]
    spread = 1 + sum(weights) // (1 << 30)
    return np.cumsum(np.array([max(1, weight // spread) for weight in weights]))


def skewed_ids(own_key, shape, count, skew):
    grid = cumulative_ranks(count, skew)
    lot = jax.random.randint(jax.random.fold_in(own_key, 1), shape, 0, int(grid[count - 1]))
    grade = jnp.searchsorted(jnp.asarray(grid, jnp.int32), lot, side="right")
    return jax.random.permutation(jax.random.fold_in(own_key, 2), count)[grade].astype(jnp.int32)


def scatter_about(own_key, shape, scale, most, shards=(), kind=jnp.bfloat16):
    array = jax.random.normal(own_key, shape, jnp.float32) * scale
    if len(shards) > 0:
        array = levels(own_key, shape, shards, -0.22, 0.18) * array
    return jnp.clip(array, min=-most, max=most).astype(kind)


def setup_inputs(seed: int = 0) -> dict:
    key_of = jax.random.split(jax.random.key(seed), 8)
    return {
        "tokens": scatter_about(key_of[0], (DOCS, SEQ, D), 1.0, 6.0, ((0, 48), (1, 16))),
        "w_in": scatter_about(key_of[1], (D, D), D ** -0.5, 0.21875),
        "factor_one": scatter_about(key_of[2], (BLK, BLK, BLK), BLK ** -0.5, 0.75, ((0, 16),)),
        "factor_two": scatter_about(key_of[3], (BLK, BLK, BLK), BLK ** -0.5, 0.75, ((0, 16),)),
        "queries": scatter_about(key_of[4], (DOCS, D), 1.0, 6.0, ((0, 48),), jnp.float32),
        "neg_ids": touch_ends(skewed_ids(key_of[5], (DOCS, NEG), DOCS, 2), jax.random.fold_in(key_of[5], 3), 0, DOCS - 1).astype(jnp.int32),
        "pad_lengths": touch_ends(jax.random.randint(key_of[6], (DOCS,), 0, SEQ // 2 + 1), jax.random.fold_in(key_of[6], 1), 0, (SEQ // 2 + 1) - 1).astype(jnp.int32),
    }


logit_scale = 20.0
epsilon = 1e-06

def rounded(value):
    return lax.optimization_barrier(value.astype(jnp.bfloat16))

def losses_of(pooled, queries, neg_ids):
    unit_doc = pooled * lax.rsqrt(lax.optimization_barrier(jnp.sum(pooled * pooled, axis=-1, keepdims=True)) + epsilon)
    unit_query = queries * lax.rsqrt(lax.optimization_barrier(jnp.sum(queries * queries, axis=-1, keepdims=True)) + epsilon)
    logits = logit_scale * jnp.dot(unit_query, unit_doc.T, precision=lax.Precision.HIGHEST)
    count = unit_doc.shape[0]
    hits = (neg_ids[:, :, None] == jnp.arange(count, dtype=jnp.int32)[None, None, :]).astype(jnp.float32)
    weight = 1.0 + lax.optimization_barrier(jnp.sum(hits, axis=1))
    total = jnp.log(lax.optimization_barrier(jnp.sum(weight * jnp.exp(logits), axis=1)))
    return total - jnp.diagonal(logits)

def mixes(document, w_in, factor_one, factor_two):
    projected = rounded(jnp.dot(document, w_in, preferred_element_type=jnp.float32))
    projected = projected.astype(jnp.float32).reshape(BLK, BLK, D)
    first_mix = rounded(jnp.einsum('ijk,ikd->ijd', factor_one.astype(jnp.float32), projected))
    second_mix = rounded(jnp.einsum('jik,kjd->ijd', factor_two.astype(jnp.float32), first_mix.astype(jnp.float32)))
    return (projected, second_mix.astype(jnp.float32))

def validity(padding):
    position = jnp.arange(SEQ, dtype=jnp.int32).reshape(BLK, BLK)
    return (position < SEQ - padding).astype(jnp.float32)[:, :, None]

def pool_one(document, padding, w_in, factor_one, factor_two):
    projected, second_mix = mixes(document, w_in, factor_one, factor_two)
    valid = validity(padding)
    squashed = jax.nn.sigmoid(projected)
    mixed = document.astype(jnp.float32).reshape(BLK, BLK, D) + projected * squashed * second_mix
    length = (SEQ - padding).astype(jnp.float32)
    return lax.optimization_barrier(jnp.sum(mixed * valid, axis=(0, 1))) / length

def grad_one(document, padding, grad_row, w_in, factor_one, factor_two):
    projected, second_mix = mixes(document, w_in, factor_one, factor_two)
    valid = validity(padding)
    length = (SEQ - padding).astype(jnp.float32)
    scaled = valid * (grad_row * (SEQ / length))[None, None, :]
    squashed = jax.nn.sigmoid(projected)
    act = projected * squashed
    slope = squashed * (1.0 + projected * (1.0 - squashed))
    grad_second = rounded(scaled * act)
    grad_gate = rounded(scaled * second_mix * slope)
    grad_first = rounded(jnp.einsum('jik,ijd->kjd', factor_two.astype(jnp.float32), grad_second.astype(jnp.float32)))
    grad_projected = rounded(jnp.einsum('ijk,ijd->ikd', factor_one.astype(jnp.float32), grad_first.astype(jnp.float32)) + grad_gate.astype(jnp.float32))
    flat = grad_projected.reshape(SEQ, D)
    return scaled.reshape(SEQ, D) + jnp.dot(flat, w_in.T, preferred_element_type=jnp.float32)

def reference(tokens, w_in, factor_one, factor_two, queries, neg_ids, pad_lengths):
    pooled = lax.map(lambda pair: pool_one(pair[0], pair[1], w_in, factor_one, factor_two), (tokens, pad_lengths))
    losses, pull = jax.vjp(lambda value: losses_of(value, queries, neg_ids), pooled)
    pooled_grad, = pull(jnp.ones_like(losses))
    tokens_grad = lax.map(lambda triple: grad_one(triple[0], triple[1], triple[2], w_in, factor_one, factor_two), (tokens, pad_lengths, pooled_grad))
    return (losses, tokens_grad)
```

```python
import functools

import jax
import jax.numpy as jnp
from jax import lax
from jax.experimental import pallas as pl
from jax.experimental.pallas import tpu as pltpu
from jax.sharding import PartitionSpec as P

logit_scale = 20.0
epsilon = 1e-06
MESH = pl.DeviceIdType.MESH
HIGHEST = lax.Precision.HIGHEST
BF16 = jnp.bfloat16
F32 = jnp.float32

NX, NYH, NC = 4, 4, 2
NS = NX * NYH
DOCS_HERE = 2
WIDTH = 768
CHUNK = 128
NCH = WIDTH // CHUNK
UNITS = DOCS_HERE * NCH
BLK = 64
SEQ = BLK * BLK
SPAN = SEQ // NS
DOCS = 96
OWNER_X = UNITS // NYH


def contract(a, b, dims, precision=None):
    return lax.dot_general(a, b, (dims, ((), ())), precision=precision, preferred_element_type=F32)


def main_kernel(
    nz,
    tokens,
    w_in,
    factor_one,
    factor_two,
    queries,
    neg_ids,
    pads,
    h_out,
    g_out,
    loss_out,
    tv,
    wv,
    f1v,
    f2v,
    nv,
    pv,
    rs,
    xb,
    rb,
    xf,
    fm,
    ff,
    hs,
    pst,
    pb,
    qb,
    qa,
    lg,
    lt,
    npad,
    wt,
    po,
    load_sem,
    fy_s,
    fy_r,
    fx_s,
    fx_r,
    fc_s,
    fc_r,
    x_s,
    x_r,
    r_s,
    r_r,
    s1_s,
    s1_r,
    h_s,
    h_r,
    q_s,
    q_r,
    qz_s,
    qz_r,
    la_s,
    la_r,
    lz_s,
    lz_r,
    chain,
):
    dp = lax.axis_index("dp")
    ctx = lax.axis_index("context")
    ylo = dp // (nz * NC)
    z = (dp // NC) % nz
    core = dp % NC
    cx, cyh = ctx // NYH, ctx % NYH

    def dp_of(ylo_, z_, core_):
        return ylo_ * (nz * NC) + z_ * NC + core_

    partner_dp = dp_of(1 - ylo, z, core)
    send_x0 = (2 * (1 - ylo) + core + 1) % NX
    own_x0 = (2 * ylo + core + 1) % NX
    own_off = (cx - own_x0 + NX) % NX
    is_owner = own_off < OWNER_X
    unit = own_off * NYH + cyh

    def owner_ctx(u):
        return ((u // NYH + send_x0) % NX) * NYH + u % NYH

    def remote(src, dst, ssem, rsem, dev):
        return pltpu.make_async_remote_copy(
            src_ref=src, dst_ref=dst, send_sem=ssem, recv_sem=rsem, device_id=dev, device_id_type=MESH
        )

    def loop(n, fn):
        def step(i, carry):
            fn(i)
            return carry

        lax.fori_loop(0, n, step, 0)

    loads = [
        pltpu.make_async_copy(src, dst, load_sem.at[i])
        for i, (src, dst) in enumerate(
            [
                (tokens, tv),
                (w_in, wv),
                (factor_one, f1v),
                (factor_two, f2v),
                (queries, qb.at[core, z, ylo]),
                (neg_ids, nv),
            ]
        )
    ]
    for cp in loads:
        cp.start()
    barrier = pltpu.get_barrier_semaphore()

    def greet(dev):
        pl.semaphore_signal(barrier, inc=1, device_id=dev, device_id_type=MESH)

    loop(NS, lambda s: greet((partner_dp, s)))
    for d in range(1, NX):
        greet((dp, ((cx + d) % NX) * NYH + cyh))
    other_core = (dp_of(ylo, z, 1 - core), ctx)
    greet(other_core)
    greet((dp_of(1 - ylo, z, 1 - core), ctx))
    greet((dp_of(ylo, (z + 1) % nz, core), ctx))
    greet((dp_of(ylo, (z + nz - 1) % nz, core), ctx))

    loads[2].wait()
    loads[3].wait()
    for pr in range(2):
        a = jnp.concatenate([f1v[2 * pr], f1v[2 * pr + 1]], axis=1)
        b = jnp.concatenate([f2v[2 * pr], f2v[2 * pr + 1]], axis=1)
        own = jnp.where(core == 0, a.astype(F32), b.astype(F32)).astype(BF16)
        hs[0, pr * BLK : (pr + 1) * BLK, :] = own
    loads[0].wait()
    loads[1].wait()
    rows = lax.broadcasted_iota(jnp.int32, (SPAN, CHUNK), 0) + ctx * SPAN
    for b in range(DOCS_HERE):
        limit = SEQ - pads[b]
        mask = (rows < limit).astype(F32)
        for c in range(0, NCH, 2):
            cols = slice(c * CHUNK, (c + 2) * CHUNK)
            p = jnp.dot(tv[b], wv[:, cols], preferred_element_type=F32).astype(BF16)
            pv[b * NCH + c] = p[:, :CHUNK]
            pv[b * NCH + c + 1] = p[:, CHUNK:]
        for c in range(NCH):
            t = tv[b, :, c * CHUNK : (c + 1) * CHUNK].astype(F32) * mask
            rs[b * NCH + c, 0:1, :] = jnp.sum(t, axis=0, keepdims=True)
            rs[b * NCH + c, 1:2, :] = jnp.full((1, CHUNK), limit, jnp.int32).astype(F32)
    loads[4].wait()
    loads[5].wait()
    mine = qb[core, z, ylo]
    qb[core, z, ylo] = mine * lax.rsqrt(jnp.sum(mine * mine, axis=-1, keepdims=True) + epsilon)

    pl.semaphore_wait(barrier, NS + NX - 1 + 4)

    def fy(t):
        return remote(
            hs.at[0, pl.ds(0, 2 * BLK)],
            ff.at[core, cx, cyh],
            fy_s.at[t],
            fy_r.at[cyh],
            (partner_dp, cx * NYH + t),
        )

    def fy_in(t):
        return remote(
            hs.at[0, pl.ds(0, 2 * BLK)], ff.at[core, cx, t], fy_s.at[t], fy_r.at[t], (partner_dp, cx * NYH + t)
        )

    loop(NYH, lambda t: fy(t).start())

    def px(u):
        return remote(pv.at[u], xb.at[ctx], x_s.at[u], x_r.at[ctx], (partner_dp, owner_ctx(u)))

    def px_in(s):
        return remote(pv.at[0], xb.at[s], x_s.at[0], x_r.at[s], (partner_dp, s))

    def pr_(u):
        return remote(rs.at[u], rb.at[ctx], r_s.at[u], r_r.at[ctx], (partner_dp, owner_ctx(u)))

    def pr_in(s):
        return remote(rs.at[0], rb.at[s], r_s.at[0], r_r.at[s], (partner_dp, s))

    def send_p(t):
        u = (t + ctx) % UNITS
        px(u).start()
        pr_(u).start()

    loop(UNITS, send_p)

    q1 = remote(qb.at[core, z, ylo], qb.at[core, z, ylo], q_s.at[0], q_r.at[0], (partner_dp, ctx))
    q1.start()

    loop(NYH, lambda t: fy_in(t).wait_recv())

    def fx(d):
        return remote(
            ff.at[core, cx], ff.at[core, cx], fx_s.at[d], fx_r.at[cx], (dp, ((cx + d + 1) % NX) * NYH + cyh)
        )

    def fx_in(d):
        o = (cx + d + 1) % NX
        return remote(ff.at[core, o], ff.at[core, o], fx_s.at[d], fx_r.at[o], (dp, o * NYH + cyh))

    loop(NX - 1, lambda d: fx(d).start())

    if nz > 1:
        for k, dist in enumerate((1, 2, 4)):
            for sgn in (dist, nz - dist):
                pl.semaphore_signal(
                    chain.at[k],
                    inc=1,
                    device_id=(dp_of(ylo, (z + sgn) % nz, core), ctx),
                    device_id_type=MESH,
                )
            pl.semaphore_wait(chain.at[k], 2)

    q1_in = remote(qb.at[core, z, 1 - ylo], qb.at[core, z, 1 - ylo], q_s.at[0], q_r.at[0], (partner_dp, ctx))
    q1_in.wait_recv()

    def qz(d):
        return remote(
            qb.at[core, z], qb.at[core, z], qz_s.at[d], qz_r.at[z], (dp_of(ylo, (z + d + 1) % nz, core), ctx)
        )

    def qz_in(d):
        o = (z + d + 1) % nz
        return remote(qb.at[core, o], qb.at[core, o], qz_s.at[d], qz_r.at[o], (dp_of(ylo, o, core), ctx))

    loop(nz - 1, lambda d: qz(d).start())

    loop(NX - 1, lambda d: fx_in(d).wait_recv())
    fc = remote(ff.at[core], ff.at[core], fc_s.at[0], fc_r.at[0], other_core)
    fc.start()

    npad[...] = jnp.full((CHUNK, CHUNK), -1.0, F32)
    npad[0:DOCS, 0:8] = nv[...].astype(F32)
    neg_t = npad[...].T
    doc_row = lax.broadcasted_iota(jnp.int32, (DOCS, CHUNK), 0)
    own_row = lax.broadcasted_iota(jnp.int32, (8, CHUNK), 0) + DOCS_HERE * dp
    weight = jnp.ones((DOCS, CHUNK), F32)
    own_weight = jnp.ones((8, CHUNK), F32)
    for n in range(8):
        line = neg_t[n : n + 1, :]
        weight = weight + (line == doc_row.astype(F32)).astype(F32)
        own_weight = own_weight + (line == own_row.astype(F32)).astype(F32)
    wt[0:DOCS, :] = weight
    wt[DOCS : DOCS + 8, :] = own_weight

    loop(nz - 1, lambda d: qz_in(d).wait_recv())
    qc = remote(qb.at[core], qb.at[core], q_s.at[1], q_r.at[1], other_core)
    qc.start()
    remote(ff.at[1 - core], ff.at[1 - core], fc_s.at[0], fc_r.at[0], other_core).wait_recv()
    remote(qb.at[1 - core], qb.at[1 - core], q_s.at[1], q_r.at[1], other_core).wait_recv()
    qa[...] = jnp.zeros_like(qa)
    for y_ in range(2):
        for z_ in range(nz):
            for c_ in range(NC):
                at = DOCS_HERE * (y_ * nz * NC + z_ * NC + c_)
                qa[at : at + DOCS_HERE, :] = qb[c_, z_, y_]

    def hsend(s):
        return remote(hs.at[s], h_out.at[unit], h_s.at[s], h_r.at[unit], (partner_dp, s))

    def s1send(s):
        return remote(pst, pb.at[unit], s1_s.at[s], s1_r.at[unit], (partner_dp, s))

    zero = jnp.zeros((BLK, CHUNK), BF16)

    def spread(a, b):
        return jnp.concatenate(
            [jnp.concatenate([a, zero], axis=1), jnp.concatenate([zero, b], axis=1)], axis=0
        )

    loop(NYH, lambda t: fy(t).wait_send())

    @pl.when(is_owner)
    def _():
        def first(s):
            px_in(s).wait_recv()
            for pr in range(2):
                a = xb[s, pr * 2 * BLK : pr * 2 * BLK + BLK, :]
                b = xb[s, pr * 2 * BLK + BLK : (pr + 1) * 2 * BLK, :]
                lhs = ff[0, s // NYH, s % NYH, pr * BLK : (pr + 1) * BLK, :]
                mixed = jnp.dot(lhs, spread(a, b), preferred_element_type=F32).astype(BF16).astype(F32)
                base = pl.multiple_of(s * SPAN + pr * 2 * BLK, 2 * BLK)
                fm[pl.ds(base, BLK), :] = mixed[:, :CHUNK]
                fm[pl.ds(base + BLK, BLK), :] = mixed[:, CHUNK:]
                xf[pl.ds(base, BLK), :] = a.astype(F32)
                xf[pl.ds(base + BLK, BLK), :] = b.astype(F32)

        loop(NS, first)
        loop(NS, lambda s: pr_in(s).wait_recv())
        sums = jnp.sum(rb[...], axis=0)
        length = rb[0, 1:2, :]
        length2 = jnp.concatenate([length, length], axis=1)
        row_pos = lax.broadcasted_iota(jnp.int32, (BLK, 2 * CHUNK), 0) * BLK + (
            lax.broadcasted_iota(jnp.int32, (BLK, 2 * CHUNK), 1) >= CHUNK
        ).astype(jnp.int32)

        def second(jp, acc):
            j0 = 2 * jp
            at0, at1 = pl.ds(j0, BLK, stride=BLK), pl.ds(j0 + 1, BLK, stride=BLK)
            lhs = ff[1, jp // (2 * NYH), (jp // 2) % NYH, pl.ds(pl.multiple_of((jp % 2) * BLK, BLK), BLK), :]
            rhs = spread(fm[at0, :].astype(BF16), fm[at1, :].astype(BF16))
            sec = jnp.dot(lhs, rhs, preferred_element_type=F32).astype(BF16).astype(F32)
            x = jnp.concatenate([xf[at0, :], xf[at1, :]], axis=1)
            sg = jax.nn.sigmoid(x)
            act = x * sg
            slope = sg * (1.0 + x * (1.0 - sg))
            valid = (row_pos + j0).astype(F32) < length2
            act = jnp.where(valid, act, 0.0)
            prod = act * sec
            for r in range(BLK // 8):
                acc = acc + prod[8 * r : 8 * r + 8, :]
            grad = contract(lhs, act.astype(BF16), ((0,), (0,))).astype(BF16).astype(F32)
            fm[at0, :] = grad[:BLK, :CHUNK]
            fm[at1, :] = grad[BLK:, CHUNK:]
            gate = jnp.where(valid, sec * slope, 0.0)
            xf[at0, :] = gate[:, :CHUNK]
            xf[at1, :] = gate[:, CHUNK:]
            return acc

        acc = lax.fori_loop(0, BLK // 2, second, jnp.zeros((8, 2 * CHUNK), F32))
        gated = jnp.sum(acc[:, :CHUNK] + acc[:, CHUNK:], axis=0, keepdims=True)
        pst[...] = (sums[0:1, :] + gated) / length
        loop(NS, lambda s: s1send(s).start())

        def third(t):
            s = (t + ctx) % NS
            for pr in range(2):
                base = pl.multiple_of(s * SPAN + pr * 2 * BLK, 2 * BLK)
                a = fm[pl.ds(base, BLK), :].astype(BF16)
                b = fm[pl.ds(base + BLK, BLK), :].astype(BF16)
                lhs = ff[0, s // NYH, s % NYH, pr * BLK : (pr + 1) * BLK, :]
                back = contract(lhs, jnp.concatenate([a, b], axis=1), ((0,), (0,)))
                lo = back[:BLK, :CHUNK] + xf[pl.ds(base, BLK), :]
                hi = back[BLK:, CHUNK:] + xf[pl.ds(base + BLK, BLK), :]
                hs[s, pr * 2 * BLK : pr * 2 * BLK + BLK, :] = lo.astype(BF16)
                hs[s, pr * 2 * BLK + BLK : (pr + 1) * 2 * BLK, :] = hi.astype(BF16)
            hsend(s).start()

        loop(NS, third)

    def s1_in(u):
        return remote(pst, pb.at[u], s1_s.at[0], s1_r.at[u], (partner_dp, owner_ctx(u)))

    loop(UNITS, lambda u: s1_in(u).wait_recv())
    po[...] = jnp.zeros_like(po)
    for b in range(DOCS_HERE):
        for c in range(NCH):
            po[b : b + 1, c * CHUNK : (c + 1) * CHUNK] = pb[b * NCH + c]
    pooled = po[...]
    scale = lax.rsqrt(jnp.sum(pooled * pooled, axis=-1, keepdims=True) + epsilon)
    unit_doc = pooled * scale
    own_logits = logit_scale * contract(unit_doc, qa[...], ((1,), (1,)), HIGHEST)
    me4 = ylo * NC + core
    lg[z, me4] = own_logits[0:DOCS_HERE, :]

    peers4 = [
        ((1 - ylo) * NC + core, (partner_dp, ctx)),
        (ylo * NC + 1 - core, other_core),
        ((1 - ylo) * NC + 1 - core, (dp_of(1 - ylo, z, 1 - core), ctx)),
    ]
    for i, (_, dev) in enumerate(peers4):
        remote(lg.at[z, me4], lg.at[z, me4], la_s.at[i], la_r.at[i], dev).start()
    for i, (slot, dev) in enumerate(peers4):
        remote(lg.at[z, slot], lg.at[z, slot], la_s.at[i], la_r.at[i], dev).wait_recv()

    def lz(d):
        return remote(lg.at[z], lg.at[z], lz_s.at[d], lz_r.at[z], (dp_of(ylo, (z + d + 1) % nz, core), ctx))

    def lz_in(d):
        o = (z + d + 1) % nz
        return remote(lg.at[o], lg.at[o], lz_s.at[d], lz_r.at[o], (dp_of(ylo, o, core), ctx))

    loop(nz - 1, lambda d: lz(d).start())
    loop(nz - 1, lambda d: lz_in(d).wait_recv())
    if nz < 12:
        lt[...] = jnp.zeros_like(lt)
    for y_ in range(2):
        for z_ in range(nz):
            for c_ in range(NC):
                at = DOCS_HERE * (y_ * nz * NC + z_ * NC + c_)
                lt[at : at + DOCS_HERE, :] = lg[z_, y_ * NC + c_]
    logits = lt[...]
    total = jnp.sum(wt[0:DOCS, :] * jnp.exp(logits), axis=0, keepdims=True)
    lane = lax.broadcasted_iota(jnp.int32, (DOCS, CHUNK), 1)
    pair = jnp.sum(jnp.where(doc_row == lane, logits, 0.0), axis=0, keepdims=True)
    losses = jnp.log(total) - pair
    own_lane = lax.broadcasted_iota(jnp.int32, (8, CHUNK), 1)
    own_pair = (own_lane == own_row).astype(F32)
    logits_grad = wt[DOCS : DOCS + 8, :] * jnp.exp(own_logits) / total - own_pair
    unit_grad = logit_scale * contract(logits_grad, qa[...], ((1,), (0,)), HIGHEST)
    inner = jnp.sum(unit_doc * unit_grad, axis=-1, keepdims=True)
    pooled_grad = scale * (unit_grad - unit_doc * inner)
    which = lax.broadcasted_iota(jnp.int32, (8, WIDTH), 0)
    lengths = jnp.where(which == 0, SEQ - pads[0], SEQ - pads[1]).astype(F32)
    g_out[...] = pooled_grad * (SEQ / lengths)
    loss_out[...] = jnp.broadcast_to(jnp.sum(own_pair * losses, axis=-1, keepdims=True), (8, CHUNK))

    def h_in(u):
        return remote(hs.at[0], h_out.at[u], h_s.at[0], h_r.at[u], (partner_dp, owner_ctx(u)))

    loop(UNITS, lambda u: h_in(u).wait_recv())

    def sent(u):
        px(u).wait_send()
        pr_(u).wait_send()

    loop(UNITS, sent)
    q1.wait_send()
    loop(NX - 1, lambda d: fx(d).wait_send())
    loop(nz - 1, lambda d: qz(d).wait_send())
    fc.wait_send()
    qc.wait_send()
    for i, (_, dev) in enumerate(peers4):
        remote(lg.at[z, me4], lg.at[z, me4], la_s.at[i], la_r.at[i], dev).wait_send()
    loop(nz - 1, lambda d: lz(d).wait_send())

    @pl.when(is_owner)
    def _():
        def done(s):
            s1send(s).wait_send()
            hsend(s).wait_send()

        loop(NS, done)


def final_kernel(h, w_in, g, losses, pads, loss_out, out):
    doc = pl.program_id(0)
    part = pl.program_id(1)
    rows = out.shape[1]
    ctx = lax.axis_index("context")
    first = ctx * SPAN + part * rows
    limit = SEQ - pads[doc]
    row = lax.broadcasted_iota(jnp.int32, (8, WIDTH), 0)
    scale = jnp.sum(jnp.where(row == doc, g[...], 0.0), axis=0, keepdims=True)
    pieces = [
        (h[c].astype(F32) * scale[:, c * CHUNK : (c + 1) * CHUNK]).astype(BF16) for c in range(NCH)
    ]
    back = contract(jnp.concatenate(pieces, axis=1), w_in[...], ((1,), (1,)))
    pos = lax.broadcasted_iota(jnp.int32, (rows, WIDTH), 0) + first
    out[0] = jnp.where(pos < limit, scale, 0.0) + back
    loss_out[0] = jnp.max(losses[0:1, :])
    loss_out[1] = jnp.max(losses[1:2, :])


def body(nz, tokens, w_in, factor_one, factor_two, queries, neg_ids, pad_lengths):
    any_ = pl.BlockSpec(memory_space=pl.ANY)
    smem = pl.BlockSpec(memory_space=pltpu.SMEM)
    vmem = pl.BlockSpec(memory_space=pltpu.VMEM)
    dma = pltpu.SemaphoreType.DMA
    nzs = max(nz - 1, 1)
    h, g, losses = pl.pallas_call(
        functools.partial(main_kernel, nz),
        out_shape=(
            jax.ShapeDtypeStruct((UNITS, SPAN, CHUNK), BF16),
            jax.ShapeDtypeStruct((8, WIDTH), F32),
            jax.ShapeDtypeStruct((8, CHUNK), F32),
        ),
        in_specs=[any_] * 6 + [smem],
        out_specs=(any_, vmem, vmem),
        scratch_shapes=[
            pltpu.VMEM((DOCS_HERE, SPAN, WIDTH), BF16),
            pltpu.VMEM((WIDTH, WIDTH), BF16),
            pltpu.VMEM((4, BLK, BLK), BF16),
            pltpu.VMEM((4, BLK, BLK), BF16),
            pltpu.VMEM((DOCS, 8), jnp.int32),
            pltpu.VMEM((UNITS, SPAN, CHUNK), BF16),
            pltpu.VMEM((UNITS, 2, CHUNK), F32),
            pltpu.VMEM((NS, SPAN, CHUNK), BF16),
            pltpu.VMEM((NS, 2, CHUNK), F32),
            pltpu.VMEM((SEQ, CHUNK), F32),
            pltpu.VMEM((SEQ, CHUNK), F32),
            pltpu.VMEM((2, NX, NYH, 2 * BLK, CHUNK), BF16),
            pltpu.VMEM((NS, SPAN, CHUNK), BF16),
            pltpu.VMEM((1, CHUNK), F32),
            pltpu.VMEM((UNITS, 1, CHUNK), F32),
            pltpu.VMEM((NC, nz, 2, DOCS_HERE, WIDTH), F32),
            pltpu.VMEM((CHUNK, WIDTH), F32),
            pltpu.VMEM((nz, 2 * NC, DOCS_HERE, CHUNK), F32),
            pltpu.VMEM((DOCS, CHUNK), F32),
            pltpu.VMEM((CHUNK, CHUNK), F32),
            pltpu.VMEM((DOCS + 8, CHUNK), F32),
            pltpu.VMEM((8, WIDTH), F32),
            dma((6,)),
            dma((NYH,)),
            dma((NYH,)),
            dma((NX - 1,)),
            dma((NX,)),
            dma((1,)),
            dma((1,)),
            dma((UNITS,)),
            dma((NS,)),
            dma((UNITS,)),
            dma((NS,)),
            dma((NS,)),
            dma((UNITS,)),
            dma((NS,)),
            dma((UNITS,)),
            dma((2,)),
            dma((2,)),
            dma((nzs,)),
            dma((nz,)),
            dma((3,)),
            dma((3,)),
            dma((nzs,)),
            dma((nz,)),
            pltpu.SemaphoreType.REGULAR((3,)),
        ],
        compiler_params=pltpu.CompilerParams(
            collective_id=0, has_side_effects=True, vmem_limit_bytes=40 * 2**20
        ),
        name="mix",
    )(tokens, w_in, factor_one, factor_two, queries, neg_ids, pad_lengths)
    parts = 2
    rows = SPAN // parts
    loss, grad = pl.pallas_call(
        final_kernel,
        grid=(DOCS_HERE, parts),
        out_shape=(
            jax.ShapeDtypeStruct((DOCS_HERE,), F32),
            jax.ShapeDtypeStruct((DOCS_HERE, SPAN, WIDTH), F32),
        ),
        in_specs=[
            pl.BlockSpec((NCH, rows, CHUNK), lambda d, p: (d, p, 0)),
            pl.BlockSpec((WIDTH, WIDTH), lambda d, p: (0, 0)),
            pl.BlockSpec((8, WIDTH), lambda d, p: (0, 0)),
            pl.BlockSpec((8, CHUNK), lambda d, p: (0, 0)),
            smem,
        ],
        out_specs=(
            smem,
            pl.BlockSpec((1, rows, WIDTH), lambda d, p: (d, p, 0)),
        ),
        compiler_params=pltpu.CompilerParams(vmem_limit_bytes=32 * 2**20),
        name="back",
    )(h, w_in, g, losses, pad_lengths)
    return (loss, grad)


def solution(mesh):
    placed = (
        P("dp", "context", None),
        P(),
        P("context", None, None),
        P("context", None, None),
        P("dp", None),
        P(),
        P("dp"),
    )
    nz = mesh.shape["dp"] // (2 * NC)
    return jax.shard_map(
        functools.partial(body, nz),
        mesh=mesh,
        in_specs=placed,
        out_specs=(P("dp"), P("dp", "context", None)),
        check_vma=False,
    )
```

```python
import functools

import jax
import jax.numpy as jnp
from jax import lax
from jax.experimental import pallas as pl
from jax.experimental.pallas import tpu as pltpu
from jax.sharding import PartitionSpec as P

logit_scale = 20.0
epsilon = 1e-06
MESH = pl.DeviceIdType.MESH
HIGHEST = lax.Precision.HIGHEST
BF16 = jnp.bfloat16
F32 = jnp.float32

NX, NYH, NC = 4, 4, 2
NS = NX * NYH
DOCS_HERE = 2
WIDTH = 768
CHUNK = 128
NCH = WIDTH // CHUNK
UNITS = DOCS_HERE * NCH
BLK = 64
SEQ = BLK * BLK
SPAN = SEQ // NS
DOCS = 96
OWNER_X = UNITS // NYH
PEERS = NS + NX - 1 + 4
EARLY = 4
UNROLL = 4
ROWS = BLK + 8


def contract(a, b, dims, precision=None):
    return lax.dot_general(a, b, (dims, ((), ())), precision=precision, preferred_element_type=F32)


def main_kernel(
    nz,
    tokens,
    w_in,
    factor_one,
    factor_two,
    queries,
    neg_ids,
    pads,
    loss_out,
    out,
    tv,
    wv,
    wtv,
    f1v,
    f2v,
    nv,
    pv,
    rs,
    xb,
    rb,
    fm,
    ac,
    sl,
    gf,
    gt,
    ff,
    ft,
    fs,
    hs,
    hb,
    ob,
    pst,
    pb,
    qb,
    qa,
    lg,
    lt,
    wt,
    po,
    load_sem,
    out_sem,
    fy_s,
    fy_r,
    fx_s,
    fx_r,
    fc_s,
    fc_r,
    x_s,
    x_r,
    r_s,
    r_r,
    s1_s,
    s1_r,
    h_s,
    h_r,
    q_s,
    q_r,
    qz_s,
    qz_r,
    la_s,
    la_r,
    lz_s,
    lz_r,
    chain,
    late,
):
    dp = lax.axis_index("dp")
    ctx = lax.axis_index("context")
    ylo = dp // (nz * NC)
    z = (dp // NC) % nz
    core = dp % NC
    cx, cyh = ctx // NYH, ctx % NYH

    def dp_of(ylo_, z_, core_):
        return ylo_ * (nz * NC) + z_ * NC + core_

    partner_dp = dp_of(1 - ylo, z, core)
    send_x0 = (2 * (1 - ylo) + core + 1) % NX
    own_x0 = (2 * ylo + core + 1) % NX
    own_off = (cx - own_x0 + NX) % NX
    is_owner = own_off < OWNER_X
    unit = own_off * NYH + cyh

    def owner_ctx(u):
        return ((u // NYH + send_x0) % NX) * NYH + u % NYH

    def remote(src, dst, ssem, rsem, dev):
        return pltpu.make_async_remote_copy(
            src_ref=src, dst_ref=dst, send_sem=ssem, recv_sem=rsem, device_id=dev, device_id_type=MESH
        )

    def loop(n, fn):
        def step(i, carry):
            fn(i)
            return carry

        lax.fori_loop(0, n, step, 0)

    loads = [
        pltpu.make_async_copy(src, dst, load_sem.at[i])
        for i, (src, dst) in enumerate(
            [
                (tokens, tv),
                (w_in, wv),
                (factor_one, f1v),
                (factor_two, f2v),
                (queries, qb.at[core, z, ylo]),
                (neg_ids, nv),
            ]
        )
    ]
    for cp in loads:
        cp.start()
    barrier = pltpu.get_barrier_semaphore()

    def greet(dev):
        pl.semaphore_signal(barrier, inc=1, device_id=dev, device_id_type=MESH)

    other_core = (dp_of(ylo, z, 1 - core), ctx)

    def each_peer(fn):
        loop(NS, lambda s: fn((partner_dp, s)))
        for d in range(1, NX):
            fn((dp, ((cx + d) % NX) * NYH + cyh))
        fn(other_core)
        fn((dp_of(1 - ylo, z, 1 - core), ctx))
        fn((dp_of(ylo, (z + 1) % nz, core), ctx))
        fn((dp_of(ylo, (z + nz - 1) % nz, core), ctx))

    is_late = (dp == 0) & (ctx == 0)
    at_corner = (dp == dp_of(0, 0, 1)) | (dp == dp_of(1, 0, 1)) | (dp == dp_of(0, 1, 0)) | (dp == dp_of(0, nz - 1, 0))
    has_late = (
        (dp == dp_of(1, 0, 0)) | ((dp == 0) & (cyh == 0) & (cx != 0)) | ((ctx == 0) & at_corner)
    )

    @pl.when(jnp.logical_not(is_late))
    def _():
        each_peer(greet)

    loads[2].wait()
    loads[3].wait()
    for pr in range(2):
        a = jnp.concatenate([f1v[2 * pr], f1v[2 * pr + 1]], axis=1)
        b = jnp.concatenate([f2v[2 * pr], f2v[2 * pr + 1]], axis=1)
        own = jnp.where(core == 0, a.astype(F32), b.astype(F32)).astype(BF16)
        fs[pr * BLK : (pr + 1) * BLK, :] = own
    def fy(t):
        return remote(
            fs,
            ff.at[core, cx, cyh],
            fy_s.at[t],
            fy_r.at[cyh],
            (partner_dp, cx * NYH + t),
        )

    def fy_in(t):
        return remote(
            fs, ff.at[core, cx, t], fy_s.at[t], fy_r.at[t], (partner_dp, cx * NYH + t)
        )


    @pl.when(is_late)
    def _():
        pl.semaphore_wait(barrier, PEERS)
        each_peer(lambda dev: pl.semaphore_signal(late, inc=1, device_id=dev, device_id_type=MESH))
        loop(NYH, lambda t: fy(t).start())

    loads[0].wait()
    loads[1].wait()
    rows = lax.broadcasted_iota(jnp.int32, (SPAN, CHUNK), 0) + ctx * SPAN
    for b in range(DOCS_HERE):
        limit = SEQ - pads[b]
        mask = (rows < limit).astype(F32)
        for c in range(0, NCH, 2):
            cols = slice(c * CHUNK, (c + 2) * CHUNK)
            p = jnp.dot(tv[b], wv[:, cols], preferred_element_type=F32).astype(BF16)
            pv[b * NCH + c] = p[:, :CHUNK]
            pv[b * NCH + c + 1] = p[:, CHUNK:]
        for c in range(NCH):
            t = tv[b, :, c * CHUNK : (c + 1) * CHUNK].astype(F32) * mask
            rs[b * NCH + c, 0:1, :] = jnp.sum(t, axis=0, keepdims=True)
            rs[b * NCH + c, 1:2, :] = jnp.full((1, CHUNK), limit, jnp.int32).astype(F32)
    loads[4].wait()
    loads[5].wait()
    mine = qb[core, z, ylo]
    qb[core, z, ylo] = mine * lax.rsqrt(jnp.sum(mine * mine, axis=-1, keepdims=True) + epsilon)

    to_late = (dp == dp_of(1, 0, 0)) & (cx == 0)

    @pl.when(jnp.logical_not(is_late | has_late))
    def _():
        pl.semaphore_wait(barrier, PEERS)

    @pl.when(has_late)
    def _():
        pl.semaphore_wait(barrier, PEERS - 1)

    @pl.when(jnp.logical_not(is_late | to_late))
    def _():
        fy(0).start()

    @pl.when(jnp.logical_not(is_late))
    def _():
        for t in range(1, NYH):
            fy(t).start()

    def px(u):
        return remote(pv.at[u], xb.at[ctx], x_s.at[u], x_r.at[ctx], (partner_dp, owner_ctx(u)))

    def px_in(s):
        return remote(pv.at[0], xb.at[s], x_s.at[0], x_r.at[s], (partner_dp, s))

    def pr_(u):
        return remote(rs.at[u], rb.at[ctx], r_s.at[u], r_r.at[ctx], (partner_dp, owner_ctx(u)))

    def pr_in(s):
        return remote(rs.at[0], rb.at[s], r_s.at[0], r_r.at[s], (partner_dp, s))

    def send_p(t):
        u = (t + ctx) % UNITS
        px(u).start()
        pr_(u).start()

    loop(EARLY, send_p)

    @pl.when(is_late | has_late)
    def _():
        loop(UNITS - EARLY, lambda t: send_p(t + EARLY))

    @pl.when(has_late)
    def _():
        pl.semaphore_wait(late, 1)

    @pl.when(to_late)
    def _():
        fy(0).start()

    q1 = remote(qb.at[core, z, ylo], qb.at[core, z, ylo], q_s.at[0], q_r.at[0], (partner_dp, ctx))
    q1.start()
    q1_in = remote(qb.at[core, z, 1 - ylo], qb.at[core, z, 1 - ylo], q_s.at[0], q_r.at[0], (partner_dp, ctx))

    def chain_say(k, dist):
        if nz > 1:
            for sgn in (dist, nz - dist):
                dev = (dp_of(ylo, (z + sgn) % nz, core), ctx)
                pl.semaphore_signal(chain.at[k], inc=1, device_id=dev, device_id_type=MESH)

    def chain_hear(k):
        if nz > 1:
            pl.semaphore_wait(chain.at[k], 2)

    chain_say(0, 1)

    doc_row = lax.broadcasted_iota(jnp.int32, (DOCS, CHUNK), 0)
    own_row = lax.broadcasted_iota(jnp.int32, (8, CHUNK), 0) + DOCS_HERE * dp
    weight = jnp.ones((DOCS, CHUNK), F32)
    own_weight = jnp.ones((8, CHUNK), F32)
    nv_lines = jnp.concatenate([nv[...], jnp.full((8, CHUNK - DOCS), -1, jnp.int32)], axis=1)
    for n in range(8):
        line = nv_lines[n : n + 1, :]
        weight = weight + (line == doc_row).astype(F32)
        own_weight = own_weight + (line == own_row).astype(F32)
    wt[0:DOCS, :] = weight
    wt[DOCS : DOCS + 8, :] = own_weight

    def fx(d):
        return remote(
            ff.at[core, cx], ff.at[core, cx], fx_s.at[d], fx_r.at[cx], (dp, ((cx + d + 1) % NX) * NYH + cyh)
        )

    def fx_in(d):
        o = (cx + d + 1) % NX
        return remote(ff.at[core, o], ff.at[core, o], fx_s.at[d], fx_r.at[o], (dp, o * NYH + cyh))

    def fc(o):
        return remote(ff.at[core, o], ff.at[core, o], fc_s.at[o], fc_r.at[o], other_core)

    def fc_in(o):
        return remote(ff.at[1 - core, o], ff.at[1 - core, o], fc_s.at[o], fc_r.at[o], other_core)

    loop(NYH, lambda t: fy_in(t).wait_recv())
    loop(NX - 1, lambda d: fx(d).start())
    fc(cx).start()

    @pl.when(jnp.logical_not(is_late | has_late))
    def _():
        loop(UNITS - EARLY, lambda t: send_p(t + EARLY))

    chain_hear(0)
    chain_say(1, 2)
    for c in range(NCH):
        wtv[c * CHUNK : (c + 1) * CHUNK, :] = wv[:, c * CHUNK : (c + 1) * CHUNK].T

    def fx_on(d):
        fx_in(d).wait_recv()
        fc((cx + d + 1) % NX).start()

    loop(NX - 1, fx_on)
    chain_hear(1)
    chain_say(2, 4)
    q1_in.wait_recv()
    chain_hear(2)

    def qz(d):
        return remote(
            qb.at[core, z], qb.at[core, z], qz_s.at[d], qz_r.at[z], (dp_of(ylo, (z + d + 1) % nz, core), ctx)
        )

    def qz_in(d):
        o = (z + d + 1) % nz
        return remote(qb.at[core, o], qb.at[core, o], qz_s.at[d], qz_r.at[o], (dp_of(ylo, o, core), ctx))

    qc = remote(qb.at[core], qb.at[core], q_s.at[1], q_r.at[1], other_core)
    loop(nz - 1, lambda d: qz(d).start())

    def pass_queries():
        loop(nz - 1, lambda d: qz_in(d).wait_recv())
        qc.start()

    loop(NX, lambda o: fc_in(o).wait_recv())

    def hsend(s):
        return remote(hs.at[s], hb.at[unit], h_s.at[s], h_r.at[unit], (partner_dp, s))

    def s1send(s):
        return remote(pst, pb.at[unit], s1_s.at[s], s1_r.at[unit], (partner_dp, s))

    zero = jnp.zeros((BLK, CHUNK), BF16)

    def spread(a, b):
        return jnp.concatenate(
            [jnp.concatenate([a, zero], axis=1), jnp.concatenate([zero, b], axis=1)], axis=0
        )

    @pl.when(is_owner)
    def _():
        here = lax.broadcasted_iota(jnp.int32, (2 * BLK, CHUNK), 0)

        def halves(s, pr):
            at = pl.multiple_of((4 * s + 2 * pr) * ROWS, 8)
            return pl.ds(at, BLK), pl.ds(pl.multiple_of(at + ROWS, 8), BLK)

        def first(t):
            s = (unit + NS - t) % NS
            px_in(s).wait_recv()
            pr_in(s).wait_recv()
            length = rb[s, 1:2, :]
            for pr in range(2):
                both = xb[s, pr * 2 * BLK : (pr + 1) * 2 * BLK, :]
                lhs = ff[0, s // NYH, s % NYH, pr * BLK : (pr + 1) * BLK, :]
                mixed = jnp.dot(lhs, spread(both[:BLK], both[BLK:]), preferred_element_type=F32)
                mixed = mixed.astype(BF16).astype(F32)
                at0, at1 = halves(s, pr)
                fm[at0, :] = mixed[:, :CHUNK]
                fm[at1, :] = mixed[:, CHUNK:]
                x = both.astype(F32)
                sg = jax.nn.sigmoid(x)
                valid = (here + (s * SPAN + pr * 2 * BLK)).astype(F32) < length
                act = jnp.where(valid, x * sg, 0.0)
                slope = jnp.where(valid, sg * (1.0 + x * (1.0 - sg)), 0.0)
                ac[at0, :] = act[:BLK]
                ac[at1, :] = act[BLK:]
                sl[at0, :] = slope[:BLK]
                sl[at1, :] = slope[BLK:]
                for f in range(2):
                    ft[f, 2 * s + pr] = ff[f, s // NYH, s % NYH, pr * BLK : (pr + 1) * BLK, :].T

        loop(NS, first)
        sums = jnp.sum(rb[...], axis=0)

        def second(step, acc):
            for k in range(UNROLL):
                jp = step * UNROLL + k
                j0 = 2 * jp
                at0, at1 = pl.ds(j0, BLK, stride=ROWS), pl.ds(j0 + 1, BLK, stride=ROWS)
                lhs = ff[1, jp // (2 * NYH), (jp // 2) % NYH, pl.ds(pl.multiple_of((jp % 2) * BLK, BLK), BLK), :]
                rhs = spread(fm[at0, :].astype(BF16), fm[at1, :].astype(BF16))
                sec = jnp.dot(lhs, rhs, preferred_element_type=F32).astype(BF16).astype(F32)
                act = jnp.concatenate([ac[at0, :], ac[at1, :]], axis=1)
                prod = act * sec
                for r in range(BLK // 8):
                    acc = acc + prod[8 * r : 8 * r + 8, :]
                grad = jnp.dot(ft[1, jp], act.astype(BF16), preferred_element_type=F32).astype(BF16).astype(F32)
                gf[at0, :] = grad[:BLK, :CHUNK]
                gf[at1, :] = grad[BLK:, CHUNK:]
                gt[at0, :] = sec[:, :CHUNK] * sl[at0, :]
                gt[at1, :] = sec[:, CHUNK:] * sl[at1, :]
            return acc

        acc = lax.fori_loop(0, BLK // 2 // UNROLL, second, jnp.zeros((8, 2 * CHUNK), F32))
        gated = jnp.sum(acc[:, :CHUNK] + acc[:, CHUNK:], axis=0, keepdims=True)
        pst[...] = (sums[0:1, :] + gated) / rb[0, 1:2, :]
        loop(NS, lambda s: s1send(s).start())

        def third(t):
            places = [(2 * t + k + ctx) % NS for k in range(2)]
            for s in places:
                for pr in range(2):
                    at0, at1 = halves(s, pr)
                    pair = jnp.concatenate([gf[at0, :], gf[at1, :]], axis=1).astype(BF16)
                    back = jnp.dot(ft[0, 2 * s + pr], pair, preferred_element_type=F32)
                    lo = back[:BLK, :CHUNK] + gt[at0, :]
                    hi = back[BLK:, CHUNK:] + gt[at1, :]
                    hs[s, pr * 2 * BLK : pr * 2 * BLK + BLK, :] = lo.astype(BF16)
                    hs[s, pr * 2 * BLK + BLK : (pr + 1) * 2 * BLK, :] = hi.astype(BF16)
            for s in places:
                hsend(s).start()

        loop(NS // 2, third)

    pass_queries()
    remote(qb.at[1 - core], qb.at[1 - core], q_s.at[1], q_r.at[1], other_core).wait_recv()
    qa[...] = jnp.zeros_like(qa)
    for y_ in range(2):
        for z_ in range(nz):
            for c_ in range(NC):
                at = DOCS_HERE * (y_ * nz * NC + z_ * NC + c_)
                qa[at : at + DOCS_HERE, :] = qb[c_, z_, y_]

    def s1_in(u):
        return remote(pst, pb.at[u], s1_s.at[0], s1_r.at[u], (partner_dp, owner_ctx(u)))

    loop(UNITS, lambda u: s1_in(u).wait_recv())
    po[...] = jnp.zeros_like(po)
    for b in range(DOCS_HERE):
        for c in range(NCH):
            po[b : b + 1, c * CHUNK : (c + 1) * CHUNK] = pb[b * NCH + c]
    pooled = po[...]
    scale = lax.rsqrt(jnp.sum(pooled * pooled, axis=-1, keepdims=True) + epsilon)
    unit_doc = pooled * scale
    own_logits = logit_scale * contract(unit_doc, qa[...], ((1,), (1,)), HIGHEST)
    me4 = ylo * NC + core
    lg[z, me4] = own_logits[0:DOCS_HERE, :]

    peers4 = [
        ((1 - ylo) * NC + core, (partner_dp, ctx)),
        (ylo * NC + 1 - core, other_core),
        ((1 - ylo) * NC + 1 - core, (dp_of(1 - ylo, z, 1 - core), ctx)),
    ]
    for i, (_, dev) in enumerate(peers4):
        remote(lg.at[z, me4], lg.at[z, me4], la_s.at[i], la_r.at[i], dev).start()
    for i, (slot, dev) in enumerate(peers4):
        remote(lg.at[z, slot], lg.at[z, slot], la_s.at[i], la_r.at[i], dev).wait_recv()

    def lz(d):
        return remote(lg.at[z], lg.at[z], lz_s.at[d], lz_r.at[z], (dp_of(ylo, (z + d + 1) % nz, core), ctx))

    def lz_in(d):
        o = (z + d + 1) % nz
        return remote(lg.at[o], lg.at[o], lz_s.at[d], lz_r.at[o], (dp_of(ylo, o, core), ctx))

    loop(nz - 1, lambda d: lz(d).start())
    loop(nz - 1, lambda d: lz_in(d).wait_recv())
    if nz < 12:
        lt[...] = jnp.zeros_like(lt)
    for y_ in range(2):
        for z_ in range(nz):
            for c_ in range(NC):
                at = DOCS_HERE * (y_ * nz * NC + z_ * NC + c_)
                lt[at : at + DOCS_HERE, :] = lg[z_, y_ * NC + c_]
    logits = lt[...]
    total = jnp.sum(wt[0:DOCS, :] * jnp.exp(logits), axis=0, keepdims=True)
    lane = lax.broadcasted_iota(jnp.int32, (DOCS, CHUNK), 1)
    pair = jnp.sum(jnp.where(doc_row == lane, logits, 0.0), axis=0, keepdims=True)
    losses = jnp.log(total) - pair
    own_lane = lax.broadcasted_iota(jnp.int32, (8, CHUNK), 1)
    own_pair = (own_lane == own_row).astype(F32)
    logits_grad = wt[DOCS : DOCS + 8, :] * jnp.exp(own_logits) / total - own_pair
    unit_grad = logit_scale * contract(logits_grad, qa[...], ((1,), (0,)), HIGHEST)
    inner = jnp.sum(unit_doc * unit_grad, axis=-1, keepdims=True)
    pooled_grad = scale * (unit_grad - unit_doc * inner)
    loss_out[...] = jnp.broadcast_to(jnp.sum(own_pair * losses, axis=-1, keepdims=True), (8, CHUNK))

    def h_in(u):
        return remote(hs.at[0], hb.at[u], h_s.at[0], h_r.at[u], (partner_dp, owner_ctx(u)))

    pos = lax.broadcasted_iota(jnp.int32, (SPAN, WIDTH), 0) + ctx * SPAN
    writes = []
    for b in range(DOCS_HERE):
        limit = SEQ - pads[b]
        grad = pooled_grad[b : b + 1, :] * (SEQ / jnp.full((1, WIDTH), limit, jnp.int32).astype(F32))
        for c in range(NCH):
            h_in(b * NCH + c).wait_recv()
        pieces = [
            (hb[b * NCH + c].astype(F32) * grad[:, c * CHUNK : (c + 1) * CHUNK]).astype(BF16) for c in range(NCH)
        ]
        back = jnp.dot(jnp.concatenate(pieces, axis=1), wtv[...], preferred_element_type=F32)
        ob[b] = jnp.where(pos < limit, grad, 0.0) + back
        writes.append(pltpu.make_async_copy(ob.at[b], out.at[b], out_sem.at[b]))
        writes[b].start()

    loop(NYH, lambda t: fy(t).wait_send())
    loop(NX, lambda o: fc(o).wait_send())

    def sent(u):
        px(u).wait_send()
        pr_(u).wait_send()

    loop(UNITS, sent)
    q1.wait_send()
    loop(NX - 1, lambda d: fx(d).wait_send())
    loop(nz - 1, lambda d: qz(d).wait_send())
    qc.wait_send()
    for i, (_, dev) in enumerate(peers4):
        remote(lg.at[z, me4], lg.at[z, me4], la_s.at[i], la_r.at[i], dev).wait_send()
    loop(nz - 1, lambda d: lz(d).wait_send())

    @pl.when(is_owner)
    def _():
        def done(s):
            s1send(s).wait_send()
            hsend(s).wait_send()

        loop(NS, done)

    for cp in writes:
        cp.wait()


def body(nz, tokens, w_in, factor_one, factor_two, queries, neg_ids, pad_lengths):
    any_ = pl.BlockSpec(memory_space=pl.ANY)
    hbm = pl.BlockSpec(memory_space=pltpu.HBM)
    smem = pl.BlockSpec(memory_space=pltpu.SMEM)
    vmem = pl.BlockSpec(memory_space=pltpu.VMEM)
    dma = pltpu.SemaphoreType.DMA
    nzs = max(nz - 1, 1)
    loss, grad = pl.pallas_call(
        functools.partial(main_kernel, nz),
        out_shape=(
            jax.ShapeDtypeStruct((8, CHUNK), F32),
            jax.ShapeDtypeStruct((DOCS_HERE, SPAN, WIDTH), F32),
        ),
        in_specs=[hbm] * 6 + [smem],
        out_specs=(vmem, any_),
        scratch_shapes=[
            pltpu.VMEM((DOCS_HERE, SPAN, WIDTH), BF16),
            pltpu.VMEM((WIDTH, WIDTH), BF16),
            pltpu.VMEM((WIDTH, WIDTH), BF16),
            pltpu.VMEM((4, BLK, BLK), BF16),
            pltpu.VMEM((4, BLK, BLK), BF16),
            pltpu.VMEM((8, DOCS), jnp.int32),
            pltpu.VMEM((UNITS, SPAN, CHUNK), BF16),
            pltpu.VMEM((UNITS, 2, CHUNK), F32),
            pltpu.VMEM((NS, SPAN, CHUNK), BF16),
            pltpu.VMEM((NS, 2, CHUNK), F32),
            pltpu.VMEM((BLK * ROWS, CHUNK), F32),
            pltpu.VMEM((BLK * ROWS, CHUNK), F32),
            pltpu.VMEM((BLK * ROWS, CHUNK), F32),
            pltpu.VMEM((BLK * ROWS, CHUNK), F32),
            pltpu.VMEM((BLK * ROWS, CHUNK), F32),
            pltpu.VMEM((2, NX, NYH, 2 * BLK, CHUNK), BF16),
            pltpu.VMEM((2, BLK // 2, 2 * BLK, BLK), BF16),
            pltpu.VMEM((2 * BLK, CHUNK), BF16),
            pltpu.VMEM((NS, SPAN, CHUNK), BF16),
            pltpu.VMEM((UNITS, SPAN, CHUNK), BF16),
            pltpu.VMEM((DOCS_HERE, SPAN, WIDTH), F32),
            pltpu.VMEM((1, CHUNK), F32),
            pltpu.VMEM((UNITS, 1, CHUNK), F32),
            pltpu.VMEM((NC, nz, 2, DOCS_HERE, WIDTH), F32),
            pltpu.VMEM((CHUNK, WIDTH), F32),
            pltpu.VMEM((nz, 2 * NC, DOCS_HERE, CHUNK), F32),
            pltpu.VMEM((DOCS, CHUNK), F32),
            pltpu.VMEM((DOCS + 8, CHUNK), F32),
            pltpu.VMEM((8, WIDTH), F32),
            dma((6,)),
            dma((DOCS_HERE,)),
            dma((NYH,)),
            dma((NYH,)),
            dma((NX - 1,)),
            dma((NX,)),
            dma((NX,)),
            dma((NX,)),
            dma((UNITS,)),
            dma((NS,)),
            dma((UNITS,)),
            dma((NS,)),
            dma((NS,)),
            dma((UNITS,)),
            dma((NS,)),
            dma((UNITS,)),
            dma((2,)),
            dma((2,)),
            dma((nzs,)),
            dma((nz,)),
            dma((3,)),
            dma((3,)),
            dma((nzs,)),
            dma((nz,)),
            pltpu.SemaphoreType.REGULAR((3,)),
            pltpu.SemaphoreType.REGULAR,
        ],
        compiler_params=pltpu.CompilerParams(
            collective_id=0, has_side_effects=True, vmem_limit_bytes=60 * 2**20
        ),
        name="mix",
    )(tokens, w_in, factor_one, factor_two, queries, neg_ids.T, pad_lengths)
    return (loss[:DOCS_HERE, 0], grad)


def solution(mesh):
    placed = (
        P("dp", "context", None),
        P(),
        P("context", None, None),
        P("context", None, None),
        P("dp", None),
        P(),
        P("dp"),
    )
    nz = mesh.shape["dp"] // (2 * NC)
    return jax.shard_map(
        functools.partial(body, nz),
        mesh=mesh,
        in_specs=placed,
        out_specs=(P("dp"), P("dp", "context", None)),
        check_vma=False,
    )
```

```python
import functools

import jax
import jax.numpy as jnp
from jax import lax
from jax.experimental import pallas as pl
from jax.experimental.pallas import tpu as pltpu
from jax.sharding import PartitionSpec as P

logit_scale = 20.0
epsilon = 1e-06
MESH = pl.DeviceIdType.MESH
HIGHEST = lax.Precision.HIGHEST
BF16 = jnp.bfloat16
F32 = jnp.float32

NX, NYH, NC = 4, 4, 2
NS = NX * NYH
DOCS_HERE = 2
WIDTH = 768
CHUNK = 128
NCH = WIDTH // CHUNK
UNITS = DOCS_HERE * NCH
BLK = 64
SEQ = BLK * BLK
SPAN = SEQ // NS
DOCS = 96
OWNER_X = UNITS // NYH
PEERS = NS + NX - 1 + 4
EARLY = 2
BACK_A, BACK_B = 4, 6
UNROLL = 4
PARTS = 2
ROWS = BLK + 8


def contract(a, b, dims, precision=None):
    return lax.dot_general(a, b, (dims, ((), ())), precision=precision, preferred_element_type=F32)


def main_kernel(
    nz,
    tokens,
    w_in,
    factor_one,
    factor_two,
    queries,
    neg_ids,
    pads,
    loss_out,
    g_out,
    hb,
    wt_out,
    tv,
    wv,
    wtv,
    f1v,
    f2v,
    nv,
    pv,
    rs,
    xb,
    rb,
    fm,
    ac,
    sl,
    gf,
    gt,
    ff,
    ft,
    fs,
    hs,
    pst,
    pb,
    qb,
    qa,
    lg,
    lt,
    wt,
    po,
    load_sem,
    out_sem,
    fy_s,
    fy_r,
    fx_s,
    fx_r,
    fc_s,
    fc_r,
    x_s,
    x_r,
    r_s,
    r_r,
    s1_s,
    s1_r,
    h_s,
    h_r,
    q_s,
    q_r,
    qz_s,
    qz_r,
    la_s,
    la_r,
    lz_s,
    lz_r,
    chain,
    late,
):
    dp = lax.axis_index("dp")
    ctx = lax.axis_index("context")
    ylo = dp // (nz * NC)
    z = (dp // NC) % nz
    core = dp % NC
    cx, cyh = ctx // NYH, ctx % NYH

    def dp_of(ylo_, z_, core_):
        return ylo_ * (nz * NC) + z_ * NC + core_

    partner_dp = dp_of(1 - ylo, z, core)
    send_x0 = (2 * (1 - ylo) + core + 1) % NX
    own_x0 = (2 * ylo + core + 1) % NX
    own_off = (cx - own_x0 + NX) % NX
    send_off = ((cx - send_x0 + NX) % NX) % OWNER_X
    is_owner = own_off < OWNER_X
    unit = own_off * NYH + cyh

    def owner_ctx(u):
        return ((u // NYH + send_x0) % NX) * NYH + u % NYH

    def remote(src, dst, ssem, rsem, dev):
        return pltpu.make_async_remote_copy(
            src_ref=src, dst_ref=dst, send_sem=ssem, recv_sem=rsem, device_id=dev, device_id_type=MESH
        )

    def loop(n, fn):
        def step(i, carry):
            fn(i)
            return carry

        lax.fori_loop(0, n, step, 0)

    loads = [
        pltpu.make_async_copy(src, dst, load_sem.at[i])
        for i, (src, dst) in enumerate(
            [
                (tokens, tv),
                (w_in, wv),
                (factor_one, f1v),
                (factor_two, f2v),
                (queries, qb.at[core, z, ylo]),
                (neg_ids, nv),
            ]
        )
    ]
    for cp in loads:
        cp.start()
    barrier = pltpu.get_barrier_semaphore()

    def greet(dev):
        pl.semaphore_signal(barrier, inc=1, device_id=dev, device_id_type=MESH)

    other_core = (dp_of(ylo, z, 1 - core), ctx)

    def each_peer(fn):
        loop(NS, lambda s: fn((partner_dp, s)))
        for d in range(1, NX):
            fn((dp, ((cx + d) % NX) * NYH + cyh))
        fn(other_core)
        fn((dp_of(1 - ylo, z, 1 - core), ctx))
        fn((dp_of(ylo, (z + 1) % nz, core), ctx))
        fn((dp_of(ylo, (z + nz - 1) % nz, core), ctx))

    is_late = (dp == 0) & (ctx == 0)
    at_corner = (dp == dp_of(0, 0, 1)) | (dp == dp_of(1, 0, 1)) | (dp == dp_of(0, 1, 0)) | (dp == dp_of(0, nz - 1, 0))
    has_late = (
        (dp == dp_of(1, 0, 0)) | ((dp == 0) & (cyh == 0) & (cx != 0)) | ((ctx == 0) & at_corner)
    )

    @pl.when(jnp.logical_not(is_late))
    def _():
        each_peer(greet)

    loads[2].wait()
    loads[3].wait()
    for pr in range(2):
        a = jnp.concatenate([f1v[2 * pr], f1v[2 * pr + 1]], axis=1)
        b = jnp.concatenate([f2v[2 * pr], f2v[2 * pr + 1]], axis=1)
        own = jnp.where(core == 0, a.astype(F32), b.astype(F32)).astype(BF16)
        fs[pr * BLK : (pr + 1) * BLK, :] = own
    def fy(t):
        return remote(
            fs,
            ff.at[core, cx, cyh],
            fy_s.at[t],
            fy_r.at[cyh],
            (partner_dp, cx * NYH + t),
        )

    def fy_in(t):
        return remote(
            fs, ff.at[core, cx, t], fy_s.at[t], fy_r.at[t], (partner_dp, cx * NYH + t)
        )


    @pl.when(is_late)
    def _():
        pl.semaphore_wait(barrier, PEERS)
        each_peer(lambda dev: pl.semaphore_signal(late, inc=1, device_id=dev, device_id_type=MESH))
        loop(NYH, lambda t: fy(t).start())

    loads[0].wait()
    loads[1].wait()
    rows = lax.broadcasted_iota(jnp.int32, (SPAN, CHUNK), 0) + ctx * SPAN
    for b in range(DOCS_HERE):
        limit = SEQ - pads[b]
        mask = (rows < limit).astype(F32)
        for c in range(0, NCH, 2):
            cols = slice(c * CHUNK, (c + 2) * CHUNK)
            p = jnp.dot(tv[b], wv[:, cols], preferred_element_type=F32).astype(BF16)
            pv[b * NCH + c] = p[:, :CHUNK]
            pv[b * NCH + c + 1] = p[:, CHUNK:]
        for c in range(NCH):
            t = tv[b, :, c * CHUNK : (c + 1) * CHUNK].astype(F32) * mask
            rs[b * NCH + c, 0:1, :] = jnp.sum(t, axis=0, keepdims=True)
            rs[b * NCH + c, 1:2, :] = jnp.full((1, CHUNK), limit, jnp.int32).astype(F32)
    loads[4].wait()
    loads[5].wait()
    mine = qb[core, z, ylo]
    qb[core, z, ylo] = mine * lax.rsqrt(jnp.sum(mine * mine, axis=-1, keepdims=True) + epsilon)

    to_late = (dp == dp_of(1, 0, 0)) & (cx == 0)

    @pl.when(jnp.logical_not(is_late | has_late))
    def _():
        pl.semaphore_wait(barrier, PEERS)

    @pl.when(has_late)
    def _():
        pl.semaphore_wait(barrier, PEERS - 1)

    @pl.when(jnp.logical_not(is_late | to_late))
    def _():
        fy(0).start()

    @pl.when(jnp.logical_not(is_late))
    def _():
        for t in range(1, NYH):
            fy(t).start()

    def px(u):
        return remote(pv.at[u], xb.at[ctx], x_s.at[u], x_r.at[ctx], (partner_dp, owner_ctx(u)))

    def px_in(s):
        return remote(pv.at[0], xb.at[s], x_s.at[0], x_r.at[s], (partner_dp, s))

    def pr_(u):
        return remote(rs.at[u], rb.at[ctx], r_s.at[u], r_r.at[ctx], (partner_dp, owner_ctx(u)))

    def pr_in(s):
        return remote(rs.at[0], rb.at[s], r_s.at[0], r_r.at[s], (partner_dp, s))

    def send_p(t):
        u = ((send_off + t // NYH) % OWNER_X) * NYH + (t + cyh) % NYH
        px(u).start()
        pr_(u).start()

    loop(EARLY, send_p)

    @pl.when(is_late | has_late)
    def _():
        loop(UNITS - EARLY, lambda t: send_p(t + EARLY))

    @pl.when(has_late)
    def _():
        pl.semaphore_wait(late, 1)

    @pl.when(to_late)
    def _():
        fy(0).start()

    q1 = remote(qb.at[core, z, ylo], qb.at[core, z, ylo], q_s.at[0], q_r.at[0], (partner_dp, ctx))
    q1.start()
    q1_in = remote(qb.at[core, z, 1 - ylo], qb.at[core, z, 1 - ylo], q_s.at[0], q_r.at[0], (partner_dp, ctx))

    def chain_say(k, dist):
        if nz > 1:
            for sgn in (dist, nz - dist):
                dev = (dp_of(ylo, (z + sgn) % nz, core), ctx)
                pl.semaphore_signal(chain.at[k], inc=1, device_id=dev, device_id_type=MESH)

    def chain_hear(k):
        if nz > 1:
            pl.semaphore_wait(chain.at[k], 2)

    chain_say(0, 1)

    doc_row = lax.broadcasted_iota(jnp.int32, (DOCS, CHUNK), 0)
    own_row = lax.broadcasted_iota(jnp.int32, (8, CHUNK), 0) + DOCS_HERE * dp
    weight = jnp.ones((DOCS, CHUNK), F32)
    own_weight = jnp.ones((8, CHUNK), F32)
    nv_lines = jnp.concatenate([nv[...], jnp.full((8, CHUNK - DOCS), -1, jnp.int32)], axis=1)
    for n in range(8):
        line = nv_lines[n : n + 1, :]
        weight = weight + (line == doc_row).astype(F32)
        own_weight = own_weight + (line == own_row).astype(F32)
    wt[0:DOCS, :] = weight
    wt[DOCS : DOCS + 8, :] = own_weight

    def fx(d):
        return remote(
            ff.at[core, cx], ff.at[core, cx], fx_s.at[d], fx_r.at[cx], (dp, ((cx + d + 1) % NX) * NYH + cyh)
        )

    def fx_in(d):
        o = (cx + d + 1) % NX
        return remote(ff.at[core, o], ff.at[core, o], fx_s.at[d], fx_r.at[o], (dp, o * NYH + cyh))

    def fc(o):
        return remote(ff.at[core, o], ff.at[core, o], fc_s.at[o], fc_r.at[o], other_core)

    def fc_in(o):
        return remote(ff.at[1 - core, o], ff.at[1 - core, o], fc_s.at[o], fc_r.at[o], other_core)

    loop(NYH, lambda t: fy_in(t).wait_recv())
    loop(NX - 1, lambda d: fx(d).start())
    fc(cx).start()

    @pl.when(jnp.logical_not(is_late | has_late))
    def _():
        loop(UNITS - EARLY, lambda t: send_p(t + EARLY))

    chain_hear(0)
    chain_say(1, 2)
    for c in range(NCH):
        wtv[c * CHUNK : (c + 1) * CHUNK, :] = wv[:, c * CHUNK : (c + 1) * CHUNK].T
    wt_write = pltpu.make_async_copy(wtv, wt_out, out_sem.at[0])
    wt_write.start()

    def fx_on(d):
        fx_in(d).wait_recv()
        fc((cx + d + 1) % NX).start()

    loop(NX - 1, fx_on)
    chain_hear(1)
    chain_say(2, 4)
    q1_in.wait_recv()
    chain_hear(2)

    def qz(d):
        return remote(
            qb.at[core, z], qb.at[core, z], qz_s.at[d], qz_r.at[z], (dp_of(ylo, (z + d + 1) % nz, core), ctx)
        )

    def qz_in(d):
        o = (z + d + 1) % nz
        return remote(qb.at[core, o], qb.at[core, o], qz_s.at[d], qz_r.at[o], (dp_of(ylo, o, core), ctx))

    qc = remote(qb.at[core], qb.at[core], q_s.at[1], q_r.at[1], other_core)
    loop(nz - 1, lambda d: qz(d).start())

    def pass_queries():
        loop(nz - 1, lambda d: qz_in(d).wait_recv())
        qc.start()

    loop(NX, lambda o: fc_in(o).wait_recv())

    def hsend(s):
        return remote(hs.at[s], hb.at[unit], h_s.at[s], h_r.at[unit], (partner_dp, s))

    def s1send(s):
        return remote(pst, pb.at[unit], s1_s.at[s], s1_r.at[unit], (partner_dp, s))

    zero = jnp.zeros((BLK, CHUNK), BF16)

    def spread(a, b):
        return jnp.concatenate(
            [jnp.concatenate([a, zero], axis=1), jnp.concatenate([zero, b], axis=1)], axis=0
        )

    def halves(s, pr):
        at = pl.multiple_of((4 * s + 2 * pr) * ROWS, 8)
        return pl.ds(at, BLK), pl.ds(pl.multiple_of(at + ROWS, 8), BLK)

    def third(t):
        places = [(2 * t + k + ctx) % NS for k in range(2)]
        for s in places:
            for pr in range(2):
                at0, at1 = halves(s, pr)
                pair = jnp.concatenate([gf[at0, :], gf[at1, :]], axis=1).astype(BF16)
                back = jnp.dot(ft[0, 2 * s + pr], pair, preferred_element_type=F32)
                lo = back[:BLK, :CHUNK] + gt[at0, :]
                hi = back[BLK:, CHUNK:] + gt[at1, :]
                hs[s, pr * 2 * BLK : pr * 2 * BLK + BLK, :] = lo.astype(BF16)
                hs[s, pr * 2 * BLK + BLK : (pr + 1) * 2 * BLK, :] = hi.astype(BF16)
        for s in places:
            hsend(s).start()

    def send_back(lo, hi):
        @pl.when(is_owner)
        def _():
            loop(hi - lo, lambda t: third(t + lo))

    @pl.when(is_owner)
    def _():
        here = lax.broadcasted_iota(jnp.int32, (2 * BLK, CHUNK), 0)

        def first(t):
            s = ((cx + NX - t // NYH) % NX) * NYH + (t + cyh) % NYH
            px_in(s).wait_recv()
            pr_in(s).wait_recv()
            length = rb[s, 1:2, :]
            for pr in range(2):
                both = xb[s, pr * 2 * BLK : (pr + 1) * 2 * BLK, :]
                lhs = ff[0, s // NYH, s % NYH, pr * BLK : (pr + 1) * BLK, :]
                mixed = jnp.dot(lhs, spread(both[:BLK], both[BLK:]), preferred_element_type=F32)
                mixed = mixed.astype(BF16).astype(F32)
                at0, at1 = halves(s, pr)
                fm[at0, :] = mixed[:, :CHUNK]
                fm[at1, :] = mixed[:, CHUNK:]
                x = both.astype(F32)
                sg = jax.nn.sigmoid(x)
                valid = (here + (s * SPAN + pr * 2 * BLK)).astype(F32) < length
                act = jnp.where(valid, x * sg, 0.0)
                slope = jnp.where(valid, sg * (1.0 + x * (1.0 - sg)), 0.0)
                ac[at0, :] = act[:BLK]
                ac[at1, :] = act[BLK:]
                sl[at0, :] = slope[:BLK]
                sl[at1, :] = slope[BLK:]
                for f in range(2):
                    ft[f, 2 * s + pr] = ff[f, s // NYH, s % NYH, pr * BLK : (pr + 1) * BLK, :].T

        loop(NS, first)
        sums = jnp.sum(rb[...], axis=0)

        def second(step, acc):
            for k in range(UNROLL):
                jp = step * UNROLL + k
                j0 = 2 * jp
                at0, at1 = pl.ds(j0, BLK, stride=ROWS), pl.ds(j0 + 1, BLK, stride=ROWS)
                lhs = ff[1, jp // (2 * NYH), (jp // 2) % NYH, pl.ds(pl.multiple_of((jp % 2) * BLK, BLK), BLK), :]
                rhs = spread(fm[at0, :].astype(BF16), fm[at1, :].astype(BF16))
                sec = jnp.dot(lhs, rhs, preferred_element_type=F32).astype(BF16).astype(F32)
                act = jnp.concatenate([ac[at0, :], ac[at1, :]], axis=1)
                prod = act * sec
                for r in range(BLK // 8):
                    acc = acc + prod[8 * r : 8 * r + 8, :]
                grad = jnp.dot(ft[1, jp], act.astype(BF16), preferred_element_type=F32).astype(BF16).astype(F32)
                gf[at0, :] = grad[:BLK, :CHUNK]
                gf[at1, :] = grad[BLK:, CHUNK:]
                gt[at0, :] = sec[:, :CHUNK] * sl[at0, :]
                gt[at1, :] = sec[:, CHUNK:] * sl[at1, :]
            return acc

        acc = lax.fori_loop(0, BLK // 2 // UNROLL, second, jnp.zeros((8, 2 * CHUNK), F32))
        gated = jnp.sum(acc[:, :CHUNK] + acc[:, CHUNK:], axis=0, keepdims=True)
        pst[...] = (sums[0:1, :] + gated) / rb[0, 1:2, :]
        loop(NS, lambda s: s1send(s).start())

    send_back(0, BACK_A)
    pass_queries()
    remote(qb.at[1 - core], qb.at[1 - core], q_s.at[1], q_r.at[1], other_core).wait_recv()
    qa[...] = jnp.zeros_like(qa)
    for y_ in range(2):
        for z_ in range(nz):
            for c_ in range(NC):
                at = DOCS_HERE * (y_ * nz * NC + z_ * NC + c_)
                qa[at : at + DOCS_HERE, :] = qb[c_, z_, y_]

    def s1_in(u):
        return remote(pst, pb.at[u], s1_s.at[0], s1_r.at[u], (partner_dp, owner_ctx(u)))

    loop(UNITS, lambda u: s1_in(u).wait_recv())
    po[...] = jnp.zeros_like(po)
    for b in range(DOCS_HERE):
        for c in range(NCH):
            po[b : b + 1, c * CHUNK : (c + 1) * CHUNK] = pb[b * NCH + c]
    pooled = po[...]
    scale = lax.rsqrt(jnp.sum(pooled * pooled, axis=-1, keepdims=True) + epsilon)
    unit_doc = pooled * scale
    own_logits = logit_scale * contract(unit_doc, qa[...], ((1,), (1,)), HIGHEST)
    me4 = ylo * NC + core
    lg[z, me4] = own_logits[0:DOCS_HERE, :]

    peers4 = [
        ((1 - ylo) * NC + core, (partner_dp, ctx)),
        (ylo * NC + 1 - core, other_core),
        ((1 - ylo) * NC + 1 - core, (dp_of(1 - ylo, z, 1 - core), ctx)),
    ]
    for i, (_, dev) in enumerate(peers4):
        remote(lg.at[z, me4], lg.at[z, me4], la_s.at[i], la_r.at[i], dev).start()
    send_back(BACK_A, BACK_B)
    for i, (slot, dev) in enumerate(peers4):
        remote(lg.at[z, slot], lg.at[z, slot], la_s.at[i], la_r.at[i], dev).wait_recv()

    def lz(d):
        return remote(lg.at[z], lg.at[z], lz_s.at[d], lz_r.at[z], (dp_of(ylo, (z + d + 1) % nz, core), ctx))

    def lz_in(d):
        o = (z + d + 1) % nz
        return remote(lg.at[o], lg.at[o], lz_s.at[d], lz_r.at[o], (dp_of(ylo, o, core), ctx))

    loop(nz - 1, lambda d: lz(d).start())
    send_back(BACK_B, NS // 2)
    loop(nz - 1, lambda d: lz_in(d).wait_recv())
    if nz < 12:
        lt[...] = jnp.zeros_like(lt)
    for y_ in range(2):
        for z_ in range(nz):
            for c_ in range(NC):
                at = DOCS_HERE * (y_ * nz * NC + z_ * NC + c_)
                lt[at : at + DOCS_HERE, :] = lg[z_, y_ * NC + c_]
    logits = lt[...]
    total = jnp.sum(wt[0:DOCS, :] * jnp.exp(logits), axis=0, keepdims=True)
    lane = lax.broadcasted_iota(jnp.int32, (DOCS, CHUNK), 1)
    pair = jnp.sum(jnp.where(doc_row == lane, logits, 0.0), axis=0, keepdims=True)
    losses = jnp.log(total) - pair
    own_lane = lax.broadcasted_iota(jnp.int32, (8, CHUNK), 1)
    own_pair = (own_lane == own_row).astype(F32)
    logits_grad = wt[DOCS : DOCS + 8, :] * jnp.exp(own_logits) / total - own_pair
    unit_grad = logit_scale * contract(logits_grad, qa[...], ((1,), (0,)), HIGHEST)
    inner = jnp.sum(unit_doc * unit_grad, axis=-1, keepdims=True)
    pooled_grad = scale * (unit_grad - unit_doc * inner)
    loss_out[...] = jnp.broadcast_to(jnp.sum(own_pair * losses, axis=-1, keepdims=True), (8, CHUNK))

    def h_in(u):
        return remote(hs.at[0], hb.at[u], h_s.at[0], h_r.at[u], (partner_dp, owner_ctx(u)))

    which = lax.broadcasted_iota(jnp.int32, (8, WIDTH), 0)
    lengths = jnp.where(which == 0, SEQ - pads[0], SEQ - pads[1]).astype(F32)
    g_out[...] = pooled_grad * (SEQ / lengths)
    loop(UNITS, lambda u: h_in(u).wait_recv())
    wt_write.wait()

    loop(NYH, lambda t: fy(t).wait_send())
    loop(NX, lambda o: fc(o).wait_send())

    def sent(u):
        px(u).wait_send()
        pr_(u).wait_send()

    loop(UNITS, sent)
    q1.wait_send()
    loop(NX - 1, lambda d: fx(d).wait_send())
    loop(nz - 1, lambda d: qz(d).wait_send())
    qc.wait_send()
    for i, (_, dev) in enumerate(peers4):
        remote(lg.at[z, me4], lg.at[z, me4], la_s.at[i], la_r.at[i], dev).wait_send()
    loop(nz - 1, lambda d: lz(d).wait_send())

    @pl.when(is_owner)
    def _():
        def done(s):
            s1send(s).wait_send()
            hsend(s).wait_send()

        loop(NS, done)


def last_kernel(losses, g, h, w_t, pads, loss_out, out, lv, gv, hv, wv, ov, load_sem, out_sem):
    first = pl.ds(0, NCH)
    second = pl.ds(NCH, NCH)
    pairs = [(g, gv), (h.at[first], hv.at[first]), (w_t, wv), (h.at[second], hv.at[second]), (losses, lv)]
    loads = [pltpu.make_async_copy(src, dst, load_sem.at[i]) for i, (src, dst) in enumerate(pairs)]
    for cp in loads:
        cp.start()
    rows = SPAN // PARTS
    pos = lax.broadcasted_iota(jnp.int32, (rows, WIDTH), 0) + lax.axis_index("context") * SPAN
    for cp in loads[:3]:
        cp.wait()
    writes = []
    for b in range(DOCS_HERE):
        if b == 1:
            loads[3].wait()
        grad = gv[b : b + 1, :]
        for k in range(PARTS):
            at = slice(k * rows, (k + 1) * rows)
            pieces = [
                (hv[b * NCH + c, at, :].astype(F32) * grad[:, c * CHUNK : (c + 1) * CHUNK]).astype(BF16)
                for c in range(NCH)
            ]
            back = jnp.dot(jnp.concatenate(pieces, axis=1), wv[...], preferred_element_type=F32)
            ov[b, at, :] = jnp.where(pos + k * rows < SEQ - pads[b], grad, 0.0) + back
            place = pl.ds(k * rows, rows)
            writes.append(pltpu.make_async_copy(ov.at[b, place], out.at[b, place], out_sem.at[b * PARTS + k]))
            writes[-1].start()
    loads[4].wait()
    for b in range(DOCS_HERE):
        loss_out[b] = jnp.max(lv[b : b + 1, :])
    for cp in writes:
        cp.wait()


def body(nz, tokens, w_in, factor_one, factor_two, queries, neg_ids, pad_lengths):
    any_ = pl.BlockSpec(memory_space=pl.ANY)
    hbm = pl.BlockSpec(memory_space=pltpu.HBM)
    smem = pl.BlockSpec(memory_space=pltpu.SMEM)
    vmem = pl.BlockSpec(memory_space=pltpu.VMEM)
    dma = pltpu.SemaphoreType.DMA
    nzs = max(nz - 1, 1)
    losses, g, h, w_t = pl.pallas_call(
        functools.partial(main_kernel, nz),
        out_shape=(
            jax.ShapeDtypeStruct((8, CHUNK), F32),
            jax.ShapeDtypeStruct((8, WIDTH), F32),
            jax.ShapeDtypeStruct((UNITS, SPAN, CHUNK), BF16),
            jax.ShapeDtypeStruct((WIDTH, WIDTH), BF16),
        ),
        in_specs=[hbm] * 6 + [smem],
        out_specs=(vmem, vmem, hbm, hbm),
        scratch_shapes=[
            pltpu.VMEM((DOCS_HERE, SPAN, WIDTH), BF16),
            pltpu.VMEM((WIDTH, WIDTH), BF16),
            pltpu.VMEM((WIDTH, WIDTH), BF16),
            pltpu.VMEM((4, BLK, BLK), BF16),
            pltpu.VMEM((4, BLK, BLK), BF16),
            pltpu.VMEM((8, DOCS), jnp.int32),
            pltpu.VMEM((UNITS, SPAN, CHUNK), BF16),
            pltpu.VMEM((UNITS, 2, CHUNK), F32),
            pltpu.VMEM((NS, SPAN, CHUNK), BF16),
            pltpu.VMEM((NS, 2, CHUNK), F32),
            pltpu.VMEM((BLK * ROWS, CHUNK), F32),
            pltpu.VMEM((BLK * ROWS, CHUNK), F32),
            pltpu.VMEM((BLK * ROWS, CHUNK), F32),
            pltpu.VMEM((BLK * ROWS, CHUNK), F32),
            pltpu.VMEM((BLK * ROWS, CHUNK), F32),
            pltpu.VMEM((2, NX, NYH, 2 * BLK, CHUNK), BF16),
            pltpu.VMEM((2, BLK // 2, 2 * BLK, BLK), BF16),
            pltpu.VMEM((2 * BLK, CHUNK), BF16),
            pltpu.VMEM((NS, SPAN, CHUNK), BF16),
            pltpu.VMEM((1, CHUNK), F32),
            pltpu.VMEM((UNITS, 1, CHUNK), F32),
            pltpu.VMEM((NC, nz, 2, DOCS_HERE, WIDTH), F32),
            pltpu.VMEM((CHUNK, WIDTH), F32),
            pltpu.VMEM((nz, 2 * NC, DOCS_HERE, CHUNK), F32),
            pltpu.VMEM((DOCS, CHUNK), F32),
            pltpu.VMEM((DOCS + 8, CHUNK), F32),
            pltpu.VMEM((8, WIDTH), F32),
            dma((6,)),
            dma((1,)),
            dma((NYH,)),
            dma((NYH,)),
            dma((NX - 1,)),
            dma((NX,)),
            dma((NX,)),
            dma((NX,)),
            dma((UNITS,)),
            dma((NS,)),
            dma((UNITS,)),
            dma((NS,)),
            dma((NS,)),
            dma((UNITS,)),
            dma((NS,)),
            dma((UNITS,)),
            dma((2,)),
            dma((2,)),
            dma((nzs,)),
            dma((nz,)),
            dma((3,)),
            dma((3,)),
            dma((nzs,)),
            dma((nz,)),
            pltpu.SemaphoreType.REGULAR((3,)),
            pltpu.SemaphoreType.REGULAR,
        ],
        compiler_params=pltpu.CompilerParams(
            collective_id=0, has_side_effects=True, vmem_limit_bytes=60 * 2**20
        ),
        name="mix",
    )(tokens, w_in, factor_one, factor_two, queries, neg_ids.T, pad_lengths)
    return pl.pallas_call(
        last_kernel,
        out_shape=(
            jax.ShapeDtypeStruct((DOCS_HERE,), F32),
            jax.ShapeDtypeStruct((DOCS_HERE, SPAN, WIDTH), F32),
        ),
        in_specs=[hbm] * 4 + [smem],
        out_specs=(smem, hbm),
        scratch_shapes=[
            pltpu.VMEM((8, CHUNK), F32),
            pltpu.VMEM((8, WIDTH), F32),
            pltpu.VMEM((UNITS, SPAN, CHUNK), BF16),
            pltpu.VMEM((WIDTH, WIDTH), BF16),
            pltpu.VMEM((DOCS_HERE, SPAN, WIDTH), F32),
            dma((5,)),
            dma((DOCS_HERE * PARTS,)),
        ],
        compiler_params=pltpu.CompilerParams(vmem_limit_bytes=60 * 2**20),
        name="back",
    )(losses, g, h, w_t, pad_lengths)


def solution(mesh):
    placed = (
        P("dp", "context", None),
        P(),
        P("context", None, None),
        P("context", None, None),
        P("dp", None),
        P(),
        P("dp"),
    )
    nz = mesh.shape["dp"] // (2 * NC)
    return jax.shard_map(
        functools.partial(body, nz),
        mesh=mesh,
        in_specs=placed,
        out_specs=(P("dp"), P("dp", "context", None)),
        check_vma=False,
    )
```

```python
import functools

import jax
import jax.numpy as jnp
from jax import lax
from jax.experimental import pallas as pl
from jax.experimental.pallas import tpu as pltpu
from jax.sharding import PartitionSpec as P

logit_scale = 20.0
epsilon = 1e-06
MESH = pl.DeviceIdType.MESH
HIGHEST = lax.Precision.HIGHEST
BF16 = jnp.bfloat16
F32 = jnp.float32

NX, NYH, NC = 4, 4, 2
NS = NX * NYH
DOCS_HERE = 2
WIDTH = 768
CHUNK = 128
NCH = WIDTH // CHUNK
UNITS = DOCS_HERE * NCH
BLK = 64
SEQ = BLK * BLK
SPAN = SEQ // NS
DOCS = 96
OWNER_X = UNITS // NYH
PEERS = NS + NX - 1 + 4
EARLY = 2
BACK_A, BACK_B = 4, 6
UNROLL = 4
PARTS = 2
ROWS = BLK + 8


def contract(a, b, dims, precision=None):
    return lax.dot_general(a, b, (dims, ((), ())), precision=precision, preferred_element_type=F32)


def main_kernel(
    nz,
    tokens,
    w_in,
    factor_one,
    factor_two,
    queries,
    neg_ids,
    pads,
    loss_out,
    g_out,
    hb,
    wt_out,
    tv,
    wv,
    wtv,
    f1v,
    f2v,
    nv,
    pv,
    rs,
    xb,
    rb,
    fm,
    ac,
    sl,
    gf,
    gt,
    ff,
    ft,
    fs,
    hs,
    pst,
    pb,
    qb,
    qa,
    lg,
    lt,
    wt,
    po,
    load_sem,
    out_sem,
    fy_s,
    fy_r,
    fx_s,
    fx_r,
    fc_s,
    fc_r,
    x_s,
    x_r,
    r_s,
    r_r,
    s1_s,
    s1_r,
    h_s,
    h_r,
    q_s,
    q_r,
    qz_s,
    qz_r,
    la_s,
    la_r,
    lz_s,
    lz_r,
    chain,
    late,
):
    dp = lax.axis_index("dp")
    ctx = lax.axis_index("context")
    ylo = dp // (nz * NC)
    z = (dp // NC) % nz
    core = dp % NC
    cx, cyh = ctx // NYH, ctx % NYH

    def dp_of(ylo_, z_, core_):
        return ylo_ * (nz * NC) + z_ * NC + core_

    partner_dp = dp_of(1 - ylo, z, core)
    send_x0 = (2 * (1 - ylo) + core + 1) % NX
    own_x0 = (2 * ylo + core + 1) % NX
    own_off = (cx - own_x0 + NX) % NX
    send_off = ((cx - send_x0 + NX) % NX) % OWNER_X
    is_owner = own_off < OWNER_X
    unit = own_off * NYH + cyh

    def owner_ctx(u):
        return ((u // NYH + send_x0) % NX) * NYH + u % NYH

    def remote(src, dst, ssem, rsem, dev):
        return pltpu.make_async_remote_copy(
            src_ref=src, dst_ref=dst, send_sem=ssem, recv_sem=rsem, device_id=dev, device_id_type=MESH
        )

    def loop(n, fn):
        def step(i, carry):
            fn(i)
            return carry

        lax.fori_loop(0, n, step, 0)

    loads = [
        pltpu.make_async_copy(src, dst, load_sem.at[i])
        for i, (src, dst) in enumerate(
            [
                (tokens, tv),
                (w_in, wv),
                (factor_one, f1v),
                (factor_two, f2v),
                (queries, qb.at[core, z, ylo]),
                (neg_ids, nv),
            ]
        )
    ]
    for cp in loads:
        cp.start()
    barrier = pltpu.get_barrier_semaphore()

    def greet(dev):
        pl.semaphore_signal(barrier, inc=1, device_id=dev, device_id_type=MESH)

    other_core = (dp_of(ylo, z, 1 - core), ctx)

    def each_peer(fn):
        loop(NS, lambda s: fn((partner_dp, s)))
        for d in range(1, NX):
            fn((dp, ((cx + d) % NX) * NYH + cyh))
        fn(other_core)
        fn((dp_of(1 - ylo, z, 1 - core), ctx))
        fn((dp_of(ylo, (z + 1) % nz, core), ctx))
        fn((dp_of(ylo, (z + nz - 1) % nz, core), ctx))

    is_late = (dp == 0) & (ctx == 0)
    at_corner = (dp == dp_of(0, 0, 1)) | (dp == dp_of(1, 0, 1)) | (dp == dp_of(0, 1, 0)) | (dp == dp_of(0, nz - 1, 0))
    has_late = (
        (dp == dp_of(1, 0, 0)) | ((dp == 0) & (cyh == 0) & (cx != 0)) | ((ctx == 0) & at_corner)
    )

    @pl.when(jnp.logical_not(is_late))
    def _():
        each_peer(greet)

    loads[2].wait()
    loads[3].wait()
    for pr in range(2):
        a = jnp.concatenate([f1v[2 * pr], f1v[2 * pr + 1]], axis=1)
        b = jnp.concatenate([f2v[2 * pr], f2v[2 * pr + 1]], axis=1)
        own = jnp.where(core == 0, a.astype(F32), b.astype(F32)).astype(BF16)
        fs[pr * BLK : (pr + 1) * BLK, :] = own
    def fy(t):
        return remote(
            fs,
            ff.at[core, cx, cyh],
            fy_s.at[t],
            fy_r.at[cyh],
            (partner_dp, cx * NYH + t),
        )

    def fy_in(t):
        return remote(
            fs, ff.at[core, cx, t], fy_s.at[t], fy_r.at[t], (partner_dp, cx * NYH + t)
        )


    @pl.when(is_late)
    def _():
        pl.semaphore_wait(barrier, PEERS)
        each_peer(lambda dev: pl.semaphore_signal(late, inc=1, device_id=dev, device_id_type=MESH))
        loop(NYH, lambda t: fy(t).start())

    loads[0].wait()
    loads[1].wait()
    rows = lax.broadcasted_iota(jnp.int32, (SPAN, CHUNK), 0) + ctx * SPAN
    for b in range(DOCS_HERE):
        limit = SEQ - pads[b]
        mask = (rows < limit).astype(F32)
        for c in range(0, NCH, 2):
            cols = slice(c * CHUNK, (c + 2) * CHUNK)
            p = jnp.dot(tv[b], wv[:, cols], preferred_element_type=F32).astype(BF16)
            pv[b * NCH + c] = p[:, :CHUNK]
            pv[b * NCH + c + 1] = p[:, CHUNK:]
        for c in range(NCH):
            t = tv[b, :, c * CHUNK : (c + 1) * CHUNK].astype(F32) * mask
            rs[b * NCH + c, 0:1, :] = jnp.sum(t, axis=0, keepdims=True)
            rs[b * NCH + c, 1:2, :] = jnp.full((1, CHUNK), limit, jnp.int32).astype(F32)
    loads[4].wait()
    loads[5].wait()
    mine = qb[core, z, ylo]
    qb[core, z, ylo] = mine * lax.rsqrt(jnp.sum(mine * mine, axis=-1, keepdims=True) + epsilon)

    to_late = (dp == dp_of(1, 0, 0)) & (cx == 0)

    @pl.when(jnp.logical_not(is_late | has_late))
    def _():
        pl.semaphore_wait(barrier, PEERS)

    @pl.when(has_late)
    def _():
        pl.semaphore_wait(barrier, PEERS - 1)

    @pl.when(jnp.logical_not(is_late | to_late))
    def _():
        fy(0).start()

    @pl.when(jnp.logical_not(is_late))
    def _():
        for t in range(1, NYH):
            fy(t).start()

    def px(u):
        return remote(pv.at[u], xb.at[ctx], x_s.at[u], x_r.at[ctx], (partner_dp, owner_ctx(u)))

    def px_in(s):
        return remote(pv.at[0], xb.at[s], x_s.at[0], x_r.at[s], (partner_dp, s))

    def pr_(u):
        return remote(rs.at[u], rb.at[ctx], r_s.at[u], r_r.at[ctx], (partner_dp, owner_ctx(u)))

    def pr_in(s):
        return remote(rs.at[0], rb.at[s], r_s.at[0], r_r.at[s], (partner_dp, s))

    def send_p(t):
        u = ((send_off + t // NYH) % OWNER_X) * NYH + (t + cyh) % NYH
        px(u).start()
        pr_(u).start()

    loop(EARLY, send_p)

    @pl.when(is_late | has_late)
    def _():
        loop(UNITS - EARLY, lambda t: send_p(t + EARLY))

    @pl.when(has_late)
    def _():
        pl.semaphore_wait(late, 1)

    @pl.when(to_late)
    def _():
        fy(0).start()

    q1 = remote(qb.at[core, z, ylo], qb.at[core, z, ylo], q_s.at[0], q_r.at[0], (partner_dp, ctx))
    q1.start()
    q1_in = remote(qb.at[core, z, 1 - ylo], qb.at[core, z, 1 - ylo], q_s.at[0], q_r.at[0], (partner_dp, ctx))

    def chain_say(k, dist):
        if nz > 1:
            for sgn in (dist, nz - dist):
                dev = (dp_of(ylo, (z + sgn) % nz, core), ctx)
                pl.semaphore_signal(chain.at[k], inc=1, device_id=dev, device_id_type=MESH)

    def chain_hear(k):
        if nz > 1:
            pl.semaphore_wait(chain.at[k], 2)

    chain_say(0, 1)

    doc_row = lax.broadcasted_iota(jnp.int32, (DOCS, CHUNK), 0)
    own_row = lax.broadcasted_iota(jnp.int32, (8, CHUNK), 0) + DOCS_HERE * dp
    weight = jnp.ones((DOCS, CHUNK), F32)
    own_weight = jnp.ones((8, CHUNK), F32)
    nv_lines = jnp.concatenate([nv[...], jnp.full((8, CHUNK - DOCS), -1, jnp.int32)], axis=1)
    for n in range(8):
        line = nv_lines[n : n + 1, :]
        weight = weight + (line == doc_row).astype(F32)
        own_weight = own_weight + (line == own_row).astype(F32)
    wt[0:DOCS, :] = weight
    wt[DOCS : DOCS + 8, :] = own_weight

    def fx(d):
        return remote(
            ff.at[core, cx], ff.at[core, cx], fx_s.at[d], fx_r.at[cx], (dp, ((cx + d + 1) % NX) * NYH + cyh)
        )

    def fx_in(d):
        o = (cx + d + 1) % NX
        return remote(ff.at[core, o], ff.at[core, o], fx_s.at[d], fx_r.at[o], (dp, o * NYH + cyh))

    def fc(o):
        return remote(ff.at[core, o], ff.at[core, o], fc_s.at[o], fc_r.at[o], other_core)

    def fc_in(o):
        return remote(ff.at[1 - core, o], ff.at[1 - core, o], fc_s.at[o], fc_r.at[o], other_core)

    def fx_piece(d, t):
        return remote(
            ff.at[core, cx, t],
            ff.at[core, cx, t],
            fx_s.at[d],
            fx_r.at[cx],
            (dp, ((cx + d + 1) % NX) * NYH + cyh),
        )

    def fy_on(t):
        fy_in(t).wait_recv()
        for d in range(NX - 1):
            fx_piece(d, t).start()

    loop(NYH, fy_on)
    fc(cx).start()

    @pl.when(jnp.logical_not(is_late | has_late))
    def _():
        loop(UNITS - EARLY, lambda t: send_p(t + EARLY))

    chain_hear(0)
    chain_say(1, 2)
    for c in range(NCH):
        wtv[c * CHUNK : (c + 1) * CHUNK, :] = wv[:, c * CHUNK : (c + 1) * CHUNK].T
    wt_write = pltpu.make_async_copy(wtv, wt_out, out_sem.at[0])
    wt_write.start()

    def fx_on(d):
        fx_in(d).wait_recv()
        fc((cx + d + 1) % NX).start()

    loop(NX - 1, fx_on)
    chain_hear(1)
    chain_say(2, 4)
    q1_in.wait_recv()
    chain_hear(2)

    def qz(d):
        return remote(
            qb.at[core, z], qb.at[core, z], qz_s.at[d], qz_r.at[z], (dp_of(ylo, (z + d + 1) % nz, core), ctx)
        )

    def qz_in(d):
        o = (z + d + 1) % nz
        return remote(qb.at[core, o], qb.at[core, o], qz_s.at[d], qz_r.at[o], (dp_of(ylo, o, core), ctx))

    qc = remote(qb.at[core], qb.at[core], q_s.at[1], q_r.at[1], other_core)
    loop(nz - 1, lambda d: qz(d).start())

    def pass_queries():
        loop(nz - 1, lambda d: qz_in(d).wait_recv())
        qc.start()

    loop(NX, lambda o: fc_in(o).wait_recv())

    def hsend(s):
        return remote(hs.at[s], hb.at[unit], h_s.at[s], h_r.at[unit], (partner_dp, s))

    def s1send(s):
        return remote(pst, pb.at[unit], s1_s.at[s], s1_r.at[unit], (partner_dp, s))

    zero = jnp.zeros((BLK, CHUNK), BF16)

    def spread(a, b):
        return jnp.concatenate(
            [jnp.concatenate([a, zero], axis=1), jnp.concatenate([zero, b], axis=1)], axis=0
        )

    def halves(s, pr):
        at = pl.multiple_of((4 * s + 2 * pr) * ROWS, 8)
        return pl.ds(at, BLK), pl.ds(pl.multiple_of(at + ROWS, 8), BLK)

    def third(t):
        places = [(2 * t + k + ctx) % NS for k in range(2)]
        for s in places:
            for pr in range(2):
                at0, at1 = halves(s, pr)
                pair = jnp.concatenate([gf[at0, :], gf[at1, :]], axis=1).astype(BF16)
                back = jnp.dot(ft[0, 2 * s + pr], pair, preferred_element_type=F32)
                lo = back[:BLK, :CHUNK] + gt[at0, :]
                hi = back[BLK:, CHUNK:] + gt[at1, :]
                hs[s, pr * 2 * BLK : pr * 2 * BLK + BLK, :] = lo.astype(BF16)
                hs[s, pr * 2 * BLK + BLK : (pr + 1) * 2 * BLK, :] = hi.astype(BF16)
        for s in places:
            hsend(s).start()

    def send_back(lo, hi):
        @pl.when(is_owner)
        def _():
            loop(hi - lo, lambda t: third(t + lo))

    @pl.when(is_owner)
    def _():
        here = lax.broadcasted_iota(jnp.int32, (2 * BLK, CHUNK), 0)

        def first(t):
            s = ((cx + NX - t // NYH) % NX) * NYH + (t + cyh) % NYH
            px_in(s).wait_recv()
            pr_in(s).wait_recv()
            length = rb[s, 1:2, :]
            for pr in range(2):
                both = xb[s, pr * 2 * BLK : (pr + 1) * 2 * BLK, :]
                lhs = ff[0, s // NYH, s % NYH, pr * BLK : (pr + 1) * BLK, :]
                mixed = jnp.dot(lhs, spread(both[:BLK], both[BLK:]), preferred_element_type=F32)
                mixed = mixed.astype(BF16).astype(F32)
                at0, at1 = halves(s, pr)
                fm[at0, :] = mixed[:, :CHUNK]
                fm[at1, :] = mixed[:, CHUNK:]
                x = both.astype(F32)
                sg = jax.nn.sigmoid(x)
                valid = (here + (s * SPAN + pr * 2 * BLK)).astype(F32) < length
                act = jnp.where(valid, x * sg, 0.0)
                slope = jnp.where(valid, sg * (1.0 + x * (1.0 - sg)), 0.0)
                ac[at0, :] = act[:BLK]
                ac[at1, :] = act[BLK:]
                sl[at0, :] = slope[:BLK]
                sl[at1, :] = slope[BLK:]
                for f in range(2):
                    ft[f, 2 * s + pr] = ff[f, s // NYH, s % NYH, pr * BLK : (pr + 1) * BLK, :].T

        loop(NS, first)
        sums = jnp.sum(rb[...], axis=0)

        def second(step, acc):
            for k in range(UNROLL):
                jp = step * UNROLL + k
                j0 = 2 * jp
                at0, at1 = pl.ds(j0, BLK, stride=ROWS), pl.ds(j0 + 1, BLK, stride=ROWS)
                lhs = ff[1, jp // (2 * NYH), (jp // 2) % NYH, pl.ds(pl.multiple_of((jp % 2) * BLK, BLK), BLK), :]
                rhs = spread(fm[at0, :].astype(BF16), fm[at1, :].astype(BF16))
                sec = jnp.dot(lhs, rhs, preferred_element_type=F32).astype(BF16).astype(F32)
                act = jnp.concatenate([ac[at0, :], ac[at1, :]], axis=1)
                prod = act * sec
                for r in range(BLK // 8):
                    acc = acc + prod[8 * r : 8 * r + 8, :]
                grad = jnp.dot(ft[1, jp], act.astype(BF16), preferred_element_type=F32).astype(BF16).astype(F32)
                gf[at0, :] = grad[:BLK, :CHUNK]
                gf[at1, :] = grad[BLK:, CHUNK:]
                gt[at0, :] = sec[:, :CHUNK] * sl[at0, :]
                gt[at1, :] = sec[:, CHUNK:] * sl[at1, :]
            return acc

        acc = lax.fori_loop(0, BLK // 2 // UNROLL, second, jnp.zeros((8, 2 * CHUNK), F32))
        gated = jnp.sum(acc[:, :CHUNK] + acc[:, CHUNK:], axis=0, keepdims=True)
        pst[...] = (sums[0:1, :] + gated) / rb[0, 1:2, :]
        loop(NS, lambda s: s1send(s).start())

    send_back(0, BACK_A)
    pass_queries()
    remote(qb.at[1 - core], qb.at[1 - core], q_s.at[1], q_r.at[1], other_core).wait_recv()
    qa[...] = jnp.zeros_like(qa)
    for y_ in range(2):
        for z_ in range(nz):
            for c_ in range(NC):
                at = DOCS_HERE * (y_ * nz * NC + z_ * NC + c_)
                qa[at : at + DOCS_HERE, :] = qb[c_, z_, y_]

    def s1_in(u):
        return remote(pst, pb.at[u], s1_s.at[0], s1_r.at[u], (partner_dp, owner_ctx(u)))

    loop(UNITS, lambda u: s1_in(u).wait_recv())
    po[...] = jnp.zeros_like(po)
    for b in range(DOCS_HERE):
        for c in range(NCH):
            po[b : b + 1, c * CHUNK : (c + 1) * CHUNK] = pb[b * NCH + c]
    pooled = po[...]
    scale = lax.rsqrt(jnp.sum(pooled * pooled, axis=-1, keepdims=True) + epsilon)
    unit_doc = pooled * scale
    own_logits = logit_scale * contract(unit_doc, qa[...], ((1,), (1,)), HIGHEST)
    me4 = ylo * NC + core
    lg[z, me4] = own_logits[0:DOCS_HERE, :]

    peers4 = [
        ((1 - ylo) * NC + core, (partner_dp, ctx)),
        (ylo * NC + 1 - core, other_core),
        ((1 - ylo) * NC + 1 - core, (dp_of(1 - ylo, z, 1 - core), ctx)),
    ]
    for i, (_, dev) in enumerate(peers4):
        remote(lg.at[z, me4], lg.at[z, me4], la_s.at[i], la_r.at[i], dev).start()
    send_back(BACK_A, BACK_B)
    for i, (slot, dev) in enumerate(peers4):
        remote(lg.at[z, slot], lg.at[z, slot], la_s.at[i], la_r.at[i], dev).wait_recv()

    def lz(d):
        return remote(lg.at[z], lg.at[z], lz_s.at[d], lz_r.at[z], (dp_of(ylo, (z + d + 1) % nz, core), ctx))

    def lz_in(d):
        o = (z + d + 1) % nz
        return remote(lg.at[o], lg.at[o], lz_s.at[d], lz_r.at[o], (dp_of(ylo, o, core), ctx))

    loop(nz - 1, lambda d: lz(d).start())
    send_back(BACK_B, NS // 2)
    loop(nz - 1, lambda d: lz_in(d).wait_recv())
    if nz < 12:
        lt[...] = jnp.zeros_like(lt)
    for y_ in range(2):
        for z_ in range(nz):
            for c_ in range(NC):
                at = DOCS_HERE * (y_ * nz * NC + z_ * NC + c_)
                lt[at : at + DOCS_HERE, :] = lg[z_, y_ * NC + c_]
    logits = lt[...]
    total = jnp.sum(wt[0:DOCS, :] * jnp.exp(logits), axis=0, keepdims=True)
    lane = lax.broadcasted_iota(jnp.int32, (DOCS, CHUNK), 1)
    pair = jnp.sum(jnp.where(doc_row == lane, logits, 0.0), axis=0, keepdims=True)
    losses = jnp.log(total) - pair
    own_lane = lax.broadcasted_iota(jnp.int32, (8, CHUNK), 1)
    own_pair = (own_lane == own_row).astype(F32)
    logits_grad = wt[DOCS : DOCS + 8, :] * jnp.exp(own_logits) / total - own_pair
    unit_grad = logit_scale * contract(logits_grad, qa[...], ((1,), (0,)), HIGHEST)
    inner = jnp.sum(unit_doc * unit_grad, axis=-1, keepdims=True)
    pooled_grad = scale * (unit_grad - unit_doc * inner)
    loss_out[...] = jnp.broadcast_to(jnp.sum(own_pair * losses, axis=-1, keepdims=True), (8, CHUNK))

    def h_in(u):
        return remote(hs.at[0], hb.at[u], h_s.at[0], h_r.at[u], (partner_dp, owner_ctx(u)))

    which = lax.broadcasted_iota(jnp.int32, (8, WIDTH), 0)
    lengths = jnp.where(which == 0, SEQ - pads[0], SEQ - pads[1]).astype(F32)
    g_out[...] = pooled_grad * (SEQ / lengths)
    loop(UNITS, lambda u: h_in(u).wait_recv())
    wt_write.wait()

    loop(NYH, lambda t: fy(t).wait_send())
    loop(NX, lambda o: fc(o).wait_send())

    def sent(u):
        px(u).wait_send()
        pr_(u).wait_send()

    loop(UNITS, sent)
    q1.wait_send()
    loop(NX - 1, lambda d: fx(d).wait_send())
    loop(nz - 1, lambda d: qz(d).wait_send())
    qc.wait_send()
    for i, (_, dev) in enumerate(peers4):
        remote(lg.at[z, me4], lg.at[z, me4], la_s.at[i], la_r.at[i], dev).wait_send()
    loop(nz - 1, lambda d: lz(d).wait_send())

    @pl.when(is_owner)
    def _():
        def done(s):
            s1send(s).wait_send()
            hsend(s).wait_send()

        loop(NS, done)


def last_kernel(losses, g, h, w_t, pads, loss_out, out, lv, gv, hv, wv, ov, load_sem, out_sem):
    first = pl.ds(0, NCH)
    second = pl.ds(NCH, NCH)
    pairs = [(g, gv), (h.at[first], hv.at[first]), (w_t, wv), (h.at[second], hv.at[second]), (losses, lv)]
    loads = [pltpu.make_async_copy(src, dst, load_sem.at[i]) for i, (src, dst) in enumerate(pairs)]
    for cp in loads:
        cp.start()
    rows = SPAN // PARTS
    pos = lax.broadcasted_iota(jnp.int32, (rows, WIDTH), 0) + lax.axis_index("context") * SPAN
    for cp in loads[:3]:
        cp.wait()
    writes = []
    for b in range(DOCS_HERE):
        if b == 1:
            loads[3].wait()
        grad = gv[b : b + 1, :]
        for k in range(PARTS):
            at = slice(k * rows, (k + 1) * rows)
            pieces = [
                (hv[b * NCH + c, at, :].astype(F32) * grad[:, c * CHUNK : (c + 1) * CHUNK]).astype(BF16)
                for c in range(NCH)
            ]
            back = jnp.dot(jnp.concatenate(pieces, axis=1), wv[...], preferred_element_type=F32)
            ov[b, at, :] = jnp.where(pos + k * rows < SEQ - pads[b], grad, 0.0) + back
            place = pl.ds(k * rows, rows)
            writes.append(pltpu.make_async_copy(ov.at[b, place], out.at[b, place], out_sem.at[b * PARTS + k]))
            writes[-1].start()
    loads[4].wait()
    for b in range(DOCS_HERE):
        loss_out[b] = jnp.max(lv[b : b + 1, :])
    for cp in writes:
        cp.wait()


def body(nz, tokens, w_in, factor_one, factor_two, queries, neg_ids, pad_lengths):
    any_ = pl.BlockSpec(memory_space=pl.ANY)
    hbm = pl.BlockSpec(memory_space=pltpu.HBM)
    smem = pl.BlockSpec(memory_space=pltpu.SMEM)
    vmem = pl.BlockSpec(memory_space=pltpu.VMEM)
    dma = pltpu.SemaphoreType.DMA
    nzs = max(nz - 1, 1)
    losses, g, h, w_t = pl.pallas_call(
        functools.partial(main_kernel, nz),
        out_shape=(
            jax.ShapeDtypeStruct((8, CHUNK), F32),
            jax.ShapeDtypeStruct((8, WIDTH), F32),
            jax.ShapeDtypeStruct((UNITS, SPAN, CHUNK), BF16),
            jax.ShapeDtypeStruct((WIDTH, WIDTH), BF16),
        ),
        in_specs=[hbm] * 6 + [smem],
        out_specs=(vmem, vmem, hbm, hbm),
        scratch_shapes=[
            pltpu.VMEM((DOCS_HERE, SPAN, WIDTH), BF16),
            pltpu.VMEM((WIDTH, WIDTH), BF16),
            pltpu.VMEM((WIDTH, WIDTH), BF16),
            pltpu.VMEM((4, BLK, BLK), BF16),
            pltpu.VMEM((4, BLK, BLK), BF16),
            pltpu.VMEM((8, DOCS), jnp.int32),
            pltpu.VMEM((UNITS, SPAN, CHUNK), BF16),
            pltpu.VMEM((UNITS, 2, CHUNK), F32),
            pltpu.VMEM((NS, SPAN, CHUNK), BF16),
            pltpu.VMEM((NS, 2, CHUNK), F32),
            pltpu.VMEM((BLK * ROWS, CHUNK), F32),
            pltpu.VMEM((BLK * ROWS, CHUNK), F32),
            pltpu.VMEM((BLK * ROWS, CHUNK), F32),
            pltpu.VMEM((BLK * ROWS, CHUNK), F32),
            pltpu.VMEM((BLK * ROWS, CHUNK), F32),
            pltpu.VMEM((2, NX, NYH, 2 * BLK, CHUNK), BF16),
            pltpu.VMEM((2, BLK // 2, 2 * BLK, BLK), BF16),
            pltpu.VMEM((2 * BLK, CHUNK), BF16),
            pltpu.VMEM((NS, SPAN, CHUNK), BF16),
            pltpu.VMEM((1, CHUNK), F32),
            pltpu.VMEM((UNITS, 1, CHUNK), F32),
            pltpu.VMEM((NC, nz, 2, DOCS_HERE, WIDTH), F32),
            pltpu.VMEM((CHUNK, WIDTH), F32),
            pltpu.VMEM((nz, 2 * NC, DOCS_HERE, CHUNK), F32),
            pltpu.VMEM((DOCS, CHUNK), F32),
            pltpu.VMEM((DOCS + 8, CHUNK), F32),
            pltpu.VMEM((8, WIDTH), F32),
            dma((6,)),
            dma((1,)),
            dma((NYH,)),
            dma((NYH,)),
            dma((NX - 1,)),
            dma((NX,)),
            dma((NX,)),
            dma((NX,)),
            dma((UNITS,)),
            dma((NS,)),
            dma((UNITS,)),
            dma((NS,)),
            dma((NS,)),
            dma((UNITS,)),
            dma((NS,)),
            dma((UNITS,)),
            dma((2,)),
            dma((2,)),
            dma((nzs,)),
            dma((nz,)),
            dma((3,)),
            dma((3,)),
            dma((nzs,)),
            dma((nz,)),
            pltpu.SemaphoreType.REGULAR((3,)),
            pltpu.SemaphoreType.REGULAR,
        ],
        compiler_params=pltpu.CompilerParams(
            collective_id=0, has_side_effects=True, vmem_limit_bytes=60 * 2**20
        ),
        name="mix",
    )(tokens, w_in, factor_one, factor_two, queries, neg_ids.T, pad_lengths)
    return pl.pallas_call(
        last_kernel,
        out_shape=(
            jax.ShapeDtypeStruct((DOCS_HERE,), F32),
            jax.ShapeDtypeStruct((DOCS_HERE, SPAN, WIDTH), F32),
        ),
        in_specs=[hbm] * 4 + [smem],
        out_specs=(smem, hbm),
        scratch_shapes=[
            pltpu.VMEM((8, CHUNK), F32),
            pltpu.VMEM((8, WIDTH), F32),
            pltpu.VMEM((UNITS, SPAN, CHUNK), BF16),
            pltpu.VMEM((WIDTH, WIDTH), BF16),
            pltpu.VMEM((DOCS_HERE, SPAN, WIDTH), F32),
            dma((5,)),
            dma((DOCS_HERE * PARTS,)),
        ],
        compiler_params=pltpu.CompilerParams(vmem_limit_bytes=60 * 2**20),
        name="back",
    )(losses, g, h, w_t, pad_lengths)


def solution(mesh):
    placed = (
        P("dp", "context", None),
        P(),
        P("context", None, None),
        P("context", None, None),
        P("dp", None),
        P(),
        P("dp"),
    )
    nz = mesh.shape["dp"] // (2 * NC)
    return jax.shard_map(
        functools.partial(body, nz),
        mesh=mesh,
        in_specs=placed,
        out_specs=(P("dp"), P("dp", "context", None)),
        check_vma=False,
    )
```
